32 devices in a mesh: frames: 16 (over z, y, x), atoms: 2 (over core).
Axes of the slice: x: 2, y: 2, z: 4, core: 2. Of those that a mesh axis runs over, the one named last changes fastest.
Arguments:
- displacements: float32 [1024, 3, 4096], P('frames', None, 'atoms'), may hold values from -2 to 2
Outputs:
- msd: float32 [4096, 1024], P(('atoms', 'frames'))
The draws below stay inside these ranges and needn't reach their ends.
All inputs are finite; a program needn't handle non-finite values.
Results may differ from the reference program's by a relative error of at most 0.0003.
Values sent between devices are 32-bit elements; how exact they have to be, the bound alone decides.
A program may use at most 64 MiB of HBM per device.

```python
import math
import jax
import jax.numpy as jnp
from jax import lax

LENGTH = 1024
ATOMS = 4096


def draw_displacements(key, part):
    key_noise = jax.random.fold_in(key, 0)
    key_weight = jax.random.fold_in(key, 2)
    key_drift = jax.random.fold_in(key, 3)
    noise = jnp.clip(jax.random.normal(key_noise, (LENGTH, 3, ATOMS), jnp.float32), -5.0, 5.0)
    scale_atom = jnp.ones((1, 1, ATOMS), jnp.float32)
    drift_size = 0.09
    index = jnp.arange(ATOMS).astype(jnp.float32)
    weight_atom = 2.0 * (index + 0.5) / ATOMS * jax.random.uniform(key_weight, (ATOMS,), jnp.float32, 0.5, 1.5)
    drift = drift_size * jnp.clip(jax.random.normal(key_drift, (LENGTH, 3, 1), jnp.float32), -4.0, 4.0)
    values = 0.03 * scale_atom * noise + drift * weight_atom[None, None, :]
    return jnp.clip(values, -2.0, 2.0).astype(jnp.float32)


def setup_inputs(seed: int = 0) -> dict:
    keys = jax.random.split(jax.random.key(seed), 2)
    displacements = draw_displacements(jax.random.fold_in(keys[1], 71), 0)
    return dict(displacements=displacements)


def reference(displacements):
    drift = jnp.sum(displacements, axis=2) / ATOMS
    positions = jnp.cumsum(displacements - drift[:, :, None], axis=0)
    squares = jnp.sum(positions * positions, axis=1)
    zero_row = jnp.zeros((1, ATOMS), squares.dtype)
    running = jnp.concatenate([zero_row, jnp.cumsum(squares, axis=0)], axis=0)
    head = running[LENGTH][None, :] - running[:LENGTH]
    tail = jnp.flip(running[1:], 0)
    width = math.gcd(ATOMS, 512)
    series = jnp.transpose(positions, (2, 1, 0)).reshape(ATOMS // width, width, 3, LENGTH)

    def correlate(block):
        spectrum = jnp.fft.rfft(block, n=2 * LENGTH, axis=-1)
        power = jnp.sum(jnp.real(spectrum) ** 2 + jnp.imag(spectrum) ** 2, axis=1)
        return jnp.fft.irfft(power, n=2 * LENGTH, axis=-1)[:, :LENGTH]

    corr = lax.map(correlate, series).reshape(ATOMS, LENGTH).astype(positions.dtype)
    counts = (LENGTH - jnp.arange(LENGTH)).astype(positions.dtype)
    return (jnp.transpose(head + tail) - 2.0 * corr) / counts[None, :]
```

```python
import functools
import math

import jax
import jax.numpy as jnp
import ml_dtypes
import numpy as np
from jax import lax
from jax.experimental import pallas as pl
from jax.experimental.pallas import tpu as pltpu
from jax.sharding import PartitionSpec as P


BLOCK = 256
LANES = 128
MESH = pl.DeviceIdType.MESH


def carried_in(array, axis, combine, identity):
    count, index = (lax.axis_size(axis), lax.axis_index(axis))
    everything = lax.all_gather(array, axis)
    start = jnp.broadcast_to(jnp.asarray(identity, array.dtype), array.shape)

    def hop(k, before):
        reached = k < index
        new = combine(before, everything[k])
        return jnp.where(reached, new, before)

    return lax.fori_loop(0, count, hop, start)


def lag_table(positions):
    length = positions.shape[0]
    count = positions.shape[3]
    series = positions.reshape(length, 3 * count)
    squares = jnp.sum(positions * positions, axis=(1, 2))
    zero_row = jnp.zeros((1, count), jnp.float32)
    running = jnp.concatenate([zero_row, jnp.cumsum(squares, axis=0)], axis=0)
    head = running[length][None, :] - running[:length]
    tail = jnp.flip(running[1:], 0)
    block = min(256, length)
    frame = jnp.arange(length, dtype=jnp.int32)
    starts = jnp.arange(0, length, block, dtype=jnp.int32)

    def add_block(corr, start):
        freq = start + jnp.arange(block, dtype=jnp.int32)
        phase = frame[:, None] * freq[None, :] % (2 * length)
        angle = phase.astype(jnp.float32) * (math.pi / length)
        cosine = jnp.cos(angle)
        sine = jnp.sin(angle)
        real_part = lax.dot_general(
            series, cosine, (((0,), (0,)), ((), ())), precision=lax.Precision.HIGHEST
        )
        imag_part = lax.dot_general(
            series, sine, (((0,), (0,)), ((), ())), precision=lax.Precision.HIGHEST
        )
        power = jnp.sum(
            (real_part * real_part + imag_part * imag_part).reshape(3, count, block), axis=0
        )
        weight = jnp.where(freq == 0, 1.0, 2.0).astype(jnp.float32) / (2.0 * length)
        term = lax.dot_general(
            power * weight[None, :],
            cosine,
            (((1,), (1,)), ((), ())),
            precision=lax.Precision.HIGHEST,
        )
        return (corr + term, None)

    corr, _ = lax.scan(add_block, jnp.zeros((count, length), jnp.float32), starts)
    parity = jnp.where(frame % 2 == 0, 1.0, -1.0).astype(jnp.float32)
    highest = jnp.dot(parity, series, precision=lax.Precision.HIGHEST)
    power_top = jnp.sum((highest * highest).reshape(3, count), axis=0)
    corr = corr + power_top[:, None] * parity[None, :] / (2.0 * length)
    counts = (length - frame).astype(jnp.float32)
    return (jnp.transpose(head + tail) - 2.0 * corr) / counts[None, :]


def add_carry(earlier, later):
    return earlier + later


def per_device(displacements):
    local_frames, _, atom_count = displacements.shape
    groups = lax.axis_size("frames")
    atom_total = atom_count * lax.axis_size("atoms")
    summed = lax.psum(jnp.sum(displacements, axis=2), "atoms")
    centred = displacements - (summed / atom_total)[:, :, None]
    partial_value = jnp.cumsum(centred, axis=0)
    earlier = carried_in(partial_value[-1], "frames", add_carry, jnp.zeros_like(partial_value[-1]))
    positions = (partial_value + earlier[None]).reshape(
        local_frames, 3, groups, atom_count // groups
    )
    return lag_table(lax.all_to_all(positions, "frames", split_axis=2, concat_axis=0, tiled=True))


def tables():
    points = 2 * BLOCK
    index = np.arange(BLOCK)
    angle = 2.0 * np.pi * (np.outer(index, index) % points) / points
    forward = np.zeros((points + 16, BLOCK))
    forward[:BLOCK] = np.cos(angle)
    forward[BLOCK:points] = -np.sin(angle)
    forward[points] = 1.0 - 2.0 * (index % 2)
    high = forward.astype(ml_dtypes.bfloat16)
    low = (forward - high.astype(np.float64)).astype(ml_dtypes.bfloat16)
    weight = np.where(index == 0, 1.0, 2.0)[None, :] / points
    inverse = np.concatenate([np.cos(angle) * weight, -np.sin(angle) * weight], axis=1)
    row, col = index[:, None], index[None, :]
    sums = np.stack([col <= row, col >= row, col <= BLOCK - 1 - row])
    return (
        np.stack([high, low]),
        sums.astype(ml_dtypes.bfloat16),
        (-2.0 * inverse).astype(np.float32),
    )


def split(value, terms):
    parts = []
    for _ in range(terms - 1):
        part = value.astype(jnp.bfloat16)
        parts.append(part)
        value = value - part.astype(jnp.float32)
    return parts + [value.astype(jnp.bfloat16)]


def mm(a, b):
    return jnp.dot(a, b, preferred_element_type=jnp.float32)


def kernel(
    groups, atom_total, x, forward, sums, inverse, out,
    xv, recv, mine, sibling, total, msgs, fv, sv, iv, drift, spectrum, acc_re, acc_im, acc_top, squares,
    load_sem, const_sem, own_sem, send_sem, recv_sem, pair_send, pair_recv, msg_send, msg_recv,
):
    me, core = lax.axis_index("frames"), lax.axis_index("atoms")
    frames = x.shape[1]
    width = recv.shape[2]
    blocks = recv.shape[1] // BLOCK
    tiles = x.shape[2] // LANES

    loads = [pltpu.make_async_copy(x.at[c], xv.at[c], load_sem.at[c]) for c in range(3)]
    for load in loads:
        load.start()
    consts = [
        pltpu.make_async_copy(src, dst, const_sem.at[i])
        for i, (src, dst) in enumerate(((forward, fv), (sums, sv), (inverse, iv)))
    ]
    for const in consts:
        const.start()

    def peer_at(k):
        return lax.rem(me + k, groups)

    def own_copy(c):
        return pltpu.make_async_copy(
            x.at[c, :, pl.ds(pl.multiple_of(me * width, width), width)],
            recv.at[c, pl.ds(pl.multiple_of(me * frames, frames), frames), :],
            own_sem.at[c],
        )

    barrier = pltpu.get_barrier_semaphore()

    def greet(k, carry):
        pl.semaphore_signal(barrier, inc=1, device_id={"frames": peer_at(k)}, device_id_type=MESH)
        return carry

    pl.semaphore_signal(barrier, inc=1, device_id={"atoms": 1 - core}, device_id_type=MESH)
    lax.fori_loop(1, groups, greet, 0)
    pl.semaphore_wait(barrier, groups)

    def far_first(t):
        return groups // 2 + (1 - 2 * lax.rem(t, 2)) * ((t + 1) // 2)

    def send_component(c):
        def send(t, carry):
            peer = peer_at(far_first(t))
            pltpu.make_async_remote_copy(
                src_ref=x.at[c, :, pl.ds(pl.multiple_of(peer * width, width), width)],
                dst_ref=recv.at[c, pl.ds(pl.multiple_of(me * frames, frames), frames), :],
                send_sem=send_sem.at[c],
                recv_sem=recv_sem.at[c],
                device_id={"frames": peer},
                device_id_type=MESH,
            ).start()
            return carry

        lax.fori_loop(0, groups - 1, send, 0)
        own_copy(c).start()

    send_component(0)

    parts = []
    for c in range(3):
        loads[c].wait()
        part = xv[c, :, 0:LANES]
        for tile in range(1, tiles):
            part = part + xv[c, :, tile * LANES : (tile + 1) * LANES]
        parts.append(part)
    lanes = mine.shape[1]
    if lanes > 3 * frames:
        parts.append(jnp.zeros((lanes - 3 * frames, LANES), jnp.float32))
    mine[...] = jnp.sum(jnp.transpose(jnp.concatenate(parts, axis=0)), axis=0, keepdims=True)
    pair = pltpu.make_async_remote_copy(
        src_ref=mine,
        dst_ref=sibling,
        send_sem=pair_send,
        recv_sem=pair_recv,
        device_id={"atoms": 1 - core},
        device_id_type=MESH,
    )
    pair.start()
    pair.wait()
    total[...] = (mine[...] + sibling[...]) / atom_total

    def tell(k):
        return pltpu.make_async_remote_copy(
            src_ref=total,
            dst_ref=msgs.at[me],
            send_sem=msg_send.at[k],
            recv_sem=msg_recv.at[k],
            device_id={"frames": peer_at(k)},
            device_id_type=MESH,
        )

    def tell_start(k, carry):
        tell(k).start()
        return carry

    lax.fori_loop(1, groups, tell_start, 0)
    send_component(1)
    send_component(2)
    msgs[pl.ds(me, 1)] = total[...][None]

    acc_re[...] = jnp.zeros_like(acc_re)
    acc_im[...] = jnp.zeros_like(acc_im)
    acc_top[...] = jnp.zeros_like(acc_top)
    squares[...] = jnp.zeros_like(squares)
    for const in consts:
        const.wait()

    def heard(k, carry):
        source = lax.rem(me + groups - k, groups)
        pltpu.make_async_remote_copy(
            src_ref=total,
            dst_ref=msgs.at[source],
            send_sem=msg_send.at[k],
            recv_sem=msg_recv.at[k],
            device_id={"frames": source},
            device_id_type=MESH,
        ).wait()
        return carry

    lax.fori_loop(1, groups, heard, 0)

    def spread(b, carry):
        column = jnp.transpose(jnp.broadcast_to(msgs[pl.ds(b, 1)][0], (LANES, lanes)))
        for c in range(3):
            drift[c, pl.ds(pl.multiple_of(b * frames, frames), frames), :] = column[
                c * frames : (c + 1) * frames
            ]
        return carry

    lax.fori_loop(0, groups, spread, 0)

    def lanes_of(value):
        return [value[:, i * width : (i + 1) * width] for i in range(blocks)]

    def component(c, carry):
        arrived = recv.at[c, pl.ds(0, (groups - 1) * frames), :]
        own_copy(c).wait()
        pltpu.make_async_copy(arrived, arrived, recv_sem.at[c]).wait()
        centred = jnp.concatenate(
            [
                recv[c, i * BLOCK : (i + 1) * BLOCK, :] - drift[c, i * BLOCK : (i + 1) * BLOCK, :]
                for i in range(blocks)
            ],
            axis=1,
        )
        high, mid, low = split(centred, 3)
        running = mm(sv[0], high) + (mm(sv[0], mid) + mm(sv[0], low))
        before = [jnp.zeros((1, width), jnp.float32)]
        for last in lanes_of(running[BLOCK - 1 : BLOCK, :])[:-1]:
            before.append(before[-1] + last)
        positions = running + jnp.concatenate(before, axis=1)
        squares[...] += positions * positions
        high, low = split(positions, 2)
        spectrum[...] = mm(fv[0], high) + (mm(fv[0], low) + mm(fv[1], high))

        def rows(r, inner):
            at = pl.ds(pl.multiple_of(r * 8, 8), 8)
            re = lanes_of(spectrum[at, :])
            im = lanes_of(spectrum[pl.ds(pl.multiple_of(BLOCK + r * 8, 8), 8), :])
            for d in range(blocks):
                here = slice(d * width, (d + 1) * width)
                real = acc_re[at, here]
                imag = acc_im[at, here]
                for i in range(blocks - d):
                    j = i + d
                    real = real + (re[i] * re[j] + im[i] * im[j])
                    if d:
                        imag = imag + (re[i] * im[j] - im[i] * re[j])
                acc_re[at, here] = real
                if d:
                    acc_im[at, here] = imag
            return inner

        lax.fori_loop(0, BLOCK // 8, rows, 0, unroll=2)
        top = lanes_of(spectrum[2 * BLOCK : 2 * BLOCK + 8, :])
        for d in range(blocks):
            here = slice(d * width, (d + 1) * width)
            value = acc_top[:, here]
            for i in range(blocks - d):
                value = value + top[i] * top[i + d]
            acc_top[:, here] = value
        return carry

    lax.fori_loop(0, 3, component, 0)

    def next_block(value):
        return jnp.concatenate([value[:, width:], jnp.zeros_like(value[:, :width])], axis=1)

    parity = (1 - 2 * (lax.broadcasted_iota(jnp.int32, (BLOCK, 1), 0) % 2)).astype(jnp.float32)
    real, imag, top = acc_re[...], acc_im[...], acc_top[0:1, :]
    cross = jnp.concatenate(
        [real + parity * next_block(real), imag + parity * next_block(imag)], axis=0
    )
    corr = jnp.dot(
        iv[...], cross, precision=lax.Precision.HIGHEST, preferred_element_type=jnp.float32
    )
    corr = corr - (top + next_block(top)) * (parity * (1.0 / BLOCK))
    parts = split(squares[...], 3)
    later = mm(sv[1], parts[0]) + (mm(sv[1], parts[1]) + mm(sv[1], parts[2]))
    parts = [jnp.concatenate(lanes_of(part)[::-1], axis=1) for part in parts]
    earlier = mm(sv[2], parts[0]) + (mm(sv[2], parts[1]) + mm(sv[2], parts[2]))
    sums_of = lanes_of(later[0:1, :])
    whole = []
    for i in range(blocks):
        value = jnp.zeros((1, width), jnp.float32)
        for j in list(range(i + 1, blocks)) + list(range(blocks - 1 - i)):
            value = value + sums_of[j]
        whole.append(value)
    result = later + earlier + jnp.concatenate(whole, axis=1) + corr
    for i, piece in enumerate(lanes_of(result)):
        out[:, i * BLOCK : (i + 1) * BLOCK] = jnp.transpose(piece)

    def sent(c, carry):
        gone = recv.at[c, pl.ds(0, (groups - 1) * frames), :]
        pltpu.make_async_copy(gone, gone, send_sem.at[c]).wait()
        return carry

    lax.fori_loop(0, 3, sent, 0)


def fused(displacements):
    frames, _, atom_count = displacements.shape
    groups = lax.axis_size("frames")
    length = frames * groups
    width = atom_count // groups
    blocks = length // BLOCK
    forward, sums, inverse = tables()
    lanes = -(-3 * frames // LANES) * LANES
    f32, bf16 = jnp.float32, jnp.bfloat16
    dma = pltpu.SemaphoreType.DMA
    numerator = pl.pallas_call(
        functools.partial(kernel, groups, atom_count * lax.axis_size("atoms")),
        out_shape=jax.ShapeDtypeStruct((width, length), f32),
        in_specs=[pl.BlockSpec(memory_space=pl.ANY)] * 4,
        out_specs=pl.BlockSpec(memory_space=pltpu.VMEM),
        scratch_shapes=[
            pltpu.VMEM((3, frames, atom_count), f32),
            pltpu.VMEM((3, length, width), f32),
            pltpu.VMEM((1, lanes), f32),
            pltpu.VMEM((1, lanes), f32),
            pltpu.VMEM((1, lanes), f32),
            pltpu.VMEM((groups, 1, lanes), f32),
            pltpu.VMEM(forward.shape, bf16),
            pltpu.VMEM(sums.shape, bf16),
            pltpu.VMEM(inverse.shape, f32),
            pltpu.VMEM((3, length, width), f32),
            pltpu.VMEM((2 * BLOCK + 16, blocks * width), f32),
            pltpu.VMEM((BLOCK, blocks * width), f32),
            pltpu.VMEM((BLOCK, blocks * width), f32),
            pltpu.VMEM((8, blocks * width), f32),
            pltpu.VMEM((BLOCK, blocks * width), f32),
            dma((3,)), dma((3,)), dma((3,)), dma((3,)), dma((3,)),
            dma, dma, dma((groups,)), dma((groups,)),
        ],
        compiler_params=pltpu.CompilerParams(
            collective_id=0, has_side_effects=True, vmem_limit_bytes=40 * 1024 * 1024
        ),
    )(jnp.transpose(displacements, (1, 0, 2)), jnp.asarray(forward), jnp.asarray(sums), jnp.asarray(inverse))
    counts = (length - jnp.arange(length)).astype(f32)
    return numerator / counts[None, :]


def fits(mesh, shape):
    groups, pairs = mesh.shape["frames"], mesh.shape["atoms"]
    length, _, atoms = shape
    frames = length // groups
    return pairs == 2 and atoms // (pairs * groups) == LANES and frames % 8 == 0 and length % BLOCK == 0


def solution(mesh):
    def run(displacements):
        return jax.shard_map(
            fused if fits(mesh, displacements.shape) else per_device,
            mesh=mesh,
            in_specs=(P("frames", None, "atoms"),),
            out_specs=P(("atoms", "frames"), None),
            check_vma=False,
        )(displacements)

    return run
```

```python
import functools
import math

import jax
import jax.numpy as jnp
import ml_dtypes
import numpy as np
from jax import lax
from jax.experimental import pallas as pl
from jax.experimental.pallas import tpu as pltpu
from jax.sharding import PartitionSpec as P


BLOCK = 256
LANES = 128
MESH = pl.DeviceIdType.MESH


def carried_in(array, axis, combine, identity):
    count, index = (lax.axis_size(axis), lax.axis_index(axis))
    everything = lax.all_gather(array, axis)
    start = jnp.broadcast_to(jnp.asarray(identity, array.dtype), array.shape)

    def hop(k, before):
        reached = k < index
        new = combine(before, everything[k])
        return jnp.where(reached, new, before)

    return lax.fori_loop(0, count, hop, start)


def lag_table(positions):
    length = positions.shape[0]
    count = positions.shape[3]
    series = positions.reshape(length, 3 * count)
    squares = jnp.sum(positions * positions, axis=(1, 2))
    zero_row = jnp.zeros((1, count), jnp.float32)
    running = jnp.concatenate([zero_row, jnp.cumsum(squares, axis=0)], axis=0)
    head = running[length][None, :] - running[:length]
    tail = jnp.flip(running[1:], 0)
    block = min(256, length)
    frame = jnp.arange(length, dtype=jnp.int32)
    starts = jnp.arange(0, length, block, dtype=jnp.int32)

    def add_block(corr, start):
        freq = start + jnp.arange(block, dtype=jnp.int32)
        phase = frame[:, None] * freq[None, :] % (2 * length)
        angle = phase.astype(jnp.float32) * (math.pi / length)
        cosine = jnp.cos(angle)
        sine = jnp.sin(angle)
        real_part = lax.dot_general(
            series, cosine, (((0,), (0,)), ((), ())), precision=lax.Precision.HIGHEST
        )
        imag_part = lax.dot_general(
            series, sine, (((0,), (0,)), ((), ())), precision=lax.Precision.HIGHEST
        )
        power = jnp.sum(
            (real_part * real_part + imag_part * imag_part).reshape(3, count, block), axis=0
        )
        weight = jnp.where(freq == 0, 1.0, 2.0).astype(jnp.float32) / (2.0 * length)
        term = lax.dot_general(
            power * weight[None, :],
            cosine,
            (((1,), (1,)), ((), ())),
            precision=lax.Precision.HIGHEST,
        )
        return (corr + term, None)

    corr, _ = lax.scan(add_block, jnp.zeros((count, length), jnp.float32), starts)
    parity = jnp.where(frame % 2 == 0, 1.0, -1.0).astype(jnp.float32)
    highest = jnp.dot(parity, series, precision=lax.Precision.HIGHEST)
    power_top = jnp.sum((highest * highest).reshape(3, count), axis=0)
    corr = corr + power_top[:, None] * parity[None, :] / (2.0 * length)
    counts = (length - frame).astype(jnp.float32)
    return (jnp.transpose(head + tail) - 2.0 * corr) / counts[None, :]


def add_carry(earlier, later):
    return earlier + later


def per_device(displacements):
    local_frames, _, atom_count = displacements.shape
    groups = lax.axis_size("frames")
    atom_total = atom_count * lax.axis_size("atoms")
    summed = lax.psum(jnp.sum(displacements, axis=2), "atoms")
    centred = displacements - (summed / atom_total)[:, :, None]
    partial_value = jnp.cumsum(centred, axis=0)
    earlier = carried_in(partial_value[-1], "frames", add_carry, jnp.zeros_like(partial_value[-1]))
    positions = (partial_value + earlier[None]).reshape(
        local_frames, 3, groups, atom_count // groups
    )
    return lag_table(lax.all_to_all(positions, "frames", split_axis=2, concat_axis=0, tiled=True))


def tables():
    points = 2 * BLOCK
    index = np.arange(BLOCK)
    angle = 2.0 * np.pi * (np.outer(index, index) % points) / points
    forward = np.zeros((points + 16, BLOCK))
    forward[:BLOCK] = np.cos(angle)
    forward[BLOCK:points] = -np.sin(angle)
    forward[points] = 1.0 - 2.0 * (index % 2)
    high = forward.astype(ml_dtypes.bfloat16)
    low = (forward - high.astype(np.float64)).astype(ml_dtypes.bfloat16)
    weight = np.where(index == 0, 1.0, 2.0)[None, :] / points
    inverse = np.concatenate([np.cos(angle) * weight, -np.sin(angle) * weight], axis=1)
    row, col = index[:, None], index[None, :]
    sums = np.stack([col <= row, col >= row, col <= BLOCK - 1 - row])
    return (
        np.stack([high, low]),
        sums.astype(ml_dtypes.bfloat16),
        (-2.0 * inverse).astype(np.float32),
    )


def split(value, terms):
    parts = []
    for _ in range(terms - 1):
        part = value.astype(jnp.bfloat16)
        parts.append(part)
        value = value - part.astype(jnp.float32)
    return parts + [value.astype(jnp.bfloat16)]


def mm(a, b):
    return jnp.dot(a, b, preferred_element_type=jnp.float32)


def kernel(
    groups, atom_total, x, forward, sums, inverse, out,
    xv, recv, mine, sibling, total, msgs, fv, sv, iv, drift, spectrum, acc_re, acc_im, acc_top, squares,
    load_sem, const_sem, own_sem, send_sem, recv_sem, pair_send, pair_recv, msg_send, msg_recv,
):
    me, core = lax.axis_index("frames"), lax.axis_index("atoms")
    frames = x.shape[1]
    width = recv.shape[2]
    blocks = recv.shape[1] // BLOCK
    tiles = x.shape[2] // LANES

    loads = [pltpu.make_async_copy(x.at[c], xv.at[c], load_sem.at[c]) for c in range(3)]
    for load in loads:
        load.start()
    consts = [
        pltpu.make_async_copy(src, dst, const_sem.at[i])
        for i, (src, dst) in enumerate(((forward, fv), (sums, sv), (inverse, iv)))
    ]
    for const in consts:
        const.start()

    def peer_at(k):
        return lax.rem(me + k, groups)

    def own_copy(c):
        return pltpu.make_async_copy(
            x.at[c, :, pl.ds(pl.multiple_of(me * width, width), width)],
            recv.at[c, pl.ds(pl.multiple_of(me * frames, frames), frames), :],
            own_sem.at[c],
        )

    barrier = pltpu.get_barrier_semaphore()

    def greet(k, carry):
        pl.semaphore_signal(barrier, inc=1, device_id={"frames": peer_at(k)}, device_id_type=MESH)
        return carry

    pl.semaphore_signal(barrier, inc=1, device_id={"atoms": 1 - core}, device_id_type=MESH)
    lax.fori_loop(1, groups, greet, 0)
    pl.semaphore_wait(barrier, groups)

    def far_first(t):
        return groups // 2 + (1 - 2 * lax.rem(t, 2)) * ((t + 1) // 2)

    def send_component(c):
        def send(t, carry):
            peer = peer_at(far_first(t))
            pltpu.make_async_remote_copy(
                src_ref=x.at[c, :, pl.ds(pl.multiple_of(peer * width, width), width)],
                dst_ref=recv.at[c, pl.ds(pl.multiple_of(me * frames, frames), frames), :],
                send_sem=send_sem.at[c],
                recv_sem=recv_sem.at[c],
                device_id={"frames": peer},
                device_id_type=MESH,
            ).start()
            return carry

        lax.fori_loop(0, groups - 1, send, 0)
        own_copy(c).start()

    send_component(0)

    parts = []
    for c in range(3):
        loads[c].wait()
        part = xv[c, :, 0:LANES]
        for tile in range(1, tiles):
            part = part + xv[c, :, tile * LANES : (tile + 1) * LANES]
        parts.append(part)
    lanes = mine.shape[1]
    if lanes > 3 * frames:
        parts.append(jnp.zeros((lanes - 3 * frames, LANES), jnp.float32))
    mine[...] = jnp.sum(jnp.transpose(jnp.concatenate(parts, axis=0)), axis=0, keepdims=True)
    pair = pltpu.make_async_remote_copy(
        src_ref=mine,
        dst_ref=sibling,
        send_sem=pair_send,
        recv_sem=pair_recv,
        device_id={"atoms": 1 - core},
        device_id_type=MESH,
    )
    pair.start()
    pair.wait()
    total[...] = (mine[...] + sibling[...]) / atom_total

    def tell(k):
        return pltpu.make_async_remote_copy(
            src_ref=total,
            dst_ref=msgs.at[me],
            send_sem=msg_send.at[k],
            recv_sem=msg_recv.at[k],
            device_id={"frames": peer_at(k)},
            device_id_type=MESH,
        )

    def tell_start(k, carry):
        tell(k).start()
        return carry

    lax.fori_loop(1, groups, tell_start, 0)
    send_component(1)
    msgs[pl.ds(me, 1)] = total[...][None]

    acc_re[...] = jnp.zeros_like(acc_re)
    acc_im[...] = jnp.zeros_like(acc_im)
    acc_top[...] = jnp.zeros_like(acc_top)
    squares[...] = jnp.zeros_like(squares)
    for const in consts:
        const.wait()

    def heard(k, carry):
        source = lax.rem(me + groups - k, groups)
        pltpu.make_async_remote_copy(
            src_ref=total,
            dst_ref=msgs.at[source],
            send_sem=msg_send.at[k],
            recv_sem=msg_recv.at[k],
            device_id={"frames": source},
            device_id_type=MESH,
        ).wait()
        return carry

    lax.fori_loop(1, groups, heard, 0)

    def spread(b, carry):
        column = jnp.transpose(jnp.broadcast_to(msgs[pl.ds(b, 1)][0], (LANES, lanes)))
        for c in range(3):
            drift[c, pl.ds(pl.multiple_of(b * frames, frames), frames), :] = column[
                c * frames : (c + 1) * frames
            ]
        return carry

    lax.fori_loop(0, groups, spread, 0)

    def sent(c):
        gone = recv.at[c, pl.ds(0, (groups - 1) * frames), :]
        pltpu.make_async_copy(gone, gone, send_sem.at[c]).wait()

    sent(0)
    send_component(2)

    def lanes_of(value):
        return [value[:, i * width : (i + 1) * width] for i in range(blocks)]

    def component(c, carry):
        arrived = recv.at[c, pl.ds(0, (groups - 1) * frames), :]
        own_copy(c).wait()
        pltpu.make_async_copy(arrived, arrived, recv_sem.at[c]).wait()
        centred = jnp.concatenate(
            [
                recv[c, i * BLOCK : (i + 1) * BLOCK, :] - drift[c, i * BLOCK : (i + 1) * BLOCK, :]
                for i in range(blocks)
            ],
            axis=1,
        )
        high, mid, low = split(centred, 3)
        running = mm(sv[0], high) + (mm(sv[0], mid) + mm(sv[0], low))
        before = [jnp.zeros((1, width), jnp.float32)]
        for last in lanes_of(running[BLOCK - 1 : BLOCK, :])[:-1]:
            before.append(before[-1] + last)
        positions = running + jnp.concatenate(before, axis=1)
        squares[...] += positions * positions
        high, low = split(positions, 2)
        spectrum[...] = mm(fv[0], high) + (mm(fv[0], low) + mm(fv[1], high))

        def rows(r, inner):
            at = pl.ds(pl.multiple_of(r * 8, 8), 8)
            re = lanes_of(spectrum[at, :])
            im = lanes_of(spectrum[pl.ds(pl.multiple_of(BLOCK + r * 8, 8), 8), :])
            for d in range(blocks):
                here = slice(d * width, (d + 1) * width)
                real = acc_re[at, here]
                imag = acc_im[at, here]
                for i in range(blocks - d):
                    j = i + d
                    real = real + (re[i] * re[j] + im[i] * im[j])
                    if d:
                        imag = imag + (re[i] * im[j] - im[i] * re[j])
                acc_re[at, here] = real
                if d:
                    acc_im[at, here] = imag
            return inner

        lax.fori_loop(0, BLOCK // 8, rows, 0, unroll=2)
        top = lanes_of(spectrum[2 * BLOCK : 2 * BLOCK + 8, :])
        for d in range(blocks):
            here = slice(d * width, (d + 1) * width)
            value = acc_top[:, here]
            for i in range(blocks - d):
                value = value + top[i] * top[i + d]
            acc_top[:, here] = value
        return carry

    lax.fori_loop(0, 3, component, 0)

    def next_block(value):
        return jnp.concatenate([value[:, width:], jnp.zeros_like(value[:, :width])], axis=1)

    parity = (1 - 2 * (lax.broadcasted_iota(jnp.int32, (BLOCK, 1), 0) % 2)).astype(jnp.float32)
    real, imag, top = acc_re[...], acc_im[...], acc_top[0:1, :]
    cross = jnp.concatenate(
        [real + parity * next_block(real), imag + parity * next_block(imag)], axis=0
    )
    corr = jnp.dot(
        iv[...], cross, precision=lax.Precision.HIGHEST, preferred_element_type=jnp.float32
    )
    corr = corr - (top + next_block(top)) * (parity * (1.0 / BLOCK))
    parts = split(squares[...], 3)
    later = mm(sv[1], parts[0]) + (mm(sv[1], parts[1]) + mm(sv[1], parts[2]))
    parts = [jnp.concatenate(lanes_of(part)[::-1], axis=1) for part in parts]
    earlier = mm(sv[2], parts[0]) + (mm(sv[2], parts[1]) + mm(sv[2], parts[2]))
    sums_of = lanes_of(later[0:1, :])
    whole = []
    for i in range(blocks):
        value = jnp.zeros((1, width), jnp.float32)
        for j in list(range(i + 1, blocks)) + list(range(blocks - 1 - i)):
            value = value + sums_of[j]
        whole.append(value)
    result = later + earlier + jnp.concatenate(whole, axis=1) + corr
    for i, piece in enumerate(lanes_of(result)):
        out[:, i * BLOCK : (i + 1) * BLOCK] = jnp.transpose(piece)

    sent(1)
    sent(2)


def fused(displacements):
    frames, _, atom_count = displacements.shape
    groups = lax.axis_size("frames")
    length = frames * groups
    width = atom_count // groups
    blocks = length // BLOCK
    forward, sums, inverse = tables()
    lanes = -(-3 * frames // LANES) * LANES
    f32, bf16 = jnp.float32, jnp.bfloat16
    dma = pltpu.SemaphoreType.DMA
    numerator = pl.pallas_call(
        functools.partial(kernel, groups, atom_count * lax.axis_size("atoms")),
        out_shape=jax.ShapeDtypeStruct((width, length), f32),
        in_specs=[pl.BlockSpec(memory_space=pltpu.HBM)] * 4,
        out_specs=pl.BlockSpec(memory_space=pltpu.VMEM),
        scratch_shapes=[
            pltpu.VMEM((3, frames, atom_count), f32),
            pltpu.VMEM((3, length, width), f32),
            pltpu.VMEM((1, lanes), f32),
            pltpu.VMEM((1, lanes), f32),
            pltpu.VMEM((1, lanes), f32),
            pltpu.VMEM((groups, 1, lanes), f32),
            pltpu.VMEM(forward.shape, bf16),
            pltpu.VMEM(sums.shape, bf16),
            pltpu.VMEM(inverse.shape, f32),
            pltpu.VMEM((3, length, width), f32),
            pltpu.VMEM((2 * BLOCK + 16, blocks * width), f32),
            pltpu.VMEM((BLOCK, blocks * width), f32),
            pltpu.VMEM((BLOCK, blocks * width), f32),
            pltpu.VMEM((8, blocks * width), f32),
            pltpu.VMEM((BLOCK, blocks * width), f32),
            dma((3,)), dma((3,)), dma((3,)), dma((3,)), dma((3,)),
            dma, dma, dma((groups,)), dma((groups,)),
        ],
        compiler_params=pltpu.CompilerParams(
            collective_id=0, has_side_effects=True, vmem_limit_bytes=60 * 1024 * 1024
        ),
    )(jnp.transpose(displacements, (1, 0, 2)), jnp.asarray(forward), jnp.asarray(sums), jnp.asarray(inverse))
    counts = (length - jnp.arange(length)).astype(f32)
    return numerator / counts[None, :]


def fits(mesh, shape):
    groups, pairs = mesh.shape["frames"], mesh.shape["atoms"]
    length, _, atoms = shape
    frames = length // groups
    return pairs == 2 and atoms // (pairs * groups) == LANES and frames % 8 == 0 and length % BLOCK == 0


def solution(mesh):
    def run(displacements):
        return jax.shard_map(
            fused if fits(mesh, displacements.shape) else per_device,
            mesh=mesh,
            in_specs=(P("frames", None, "atoms"),),
            out_specs=P(("atoms", "frames"), None),
            check_vma=False,
        )(displacements)

    return run
```

```python
import functools
import math

import jax
import jax.numpy as jnp
import ml_dtypes
import numpy as np
from jax import lax
from jax.experimental import pallas as pl
from jax.experimental.pallas import tpu as pltpu
from jax.sharding import PartitionSpec as P


BLOCK = 256
LANES = 128
MESH = pl.DeviceIdType.MESH


def carried_in(array, axis, combine, identity):
    count, index = (lax.axis_size(axis), lax.axis_index(axis))
    everything = lax.all_gather(array, axis)
    start = jnp.broadcast_to(jnp.asarray(identity, array.dtype), array.shape)

    def hop(k, before):
        reached = k < index
        new = combine(before, everything[k])
        return jnp.where(reached, new, before)

    return lax.fori_loop(0, count, hop, start)


def lag_table(positions):
    length = positions.shape[0]
    count = positions.shape[3]
    series = positions.reshape(length, 3 * count)
    squares = jnp.sum(positions * positions, axis=(1, 2))
    zero_row = jnp.zeros((1, count), jnp.float32)
    running = jnp.concatenate([zero_row, jnp.cumsum(squares, axis=0)], axis=0)
    head = running[length][None, :] - running[:length]
    tail = jnp.flip(running[1:], 0)
    block = min(256, length)
    frame = jnp.arange(length, dtype=jnp.int32)
    starts = jnp.arange(0, length, block, dtype=jnp.int32)

    def add_block(corr, start):
        freq = start + jnp.arange(block, dtype=jnp.int32)
        phase = frame[:, None] * freq[None, :] % (2 * length)
        angle = phase.astype(jnp.float32) * (math.pi / length)
        cosine = jnp.cos(angle)
        sine = jnp.sin(angle)
        real_part = lax.dot_general(
            series, cosine, (((0,), (0,)), ((), ())), precision=lax.Precision.HIGHEST
        )
        imag_part = lax.dot_general(
            series, sine, (((0,), (0,)), ((), ())), precision=lax.Precision.HIGHEST
        )
        power = jnp.sum(
            (real_part * real_part + imag_part * imag_part).reshape(3, count, block), axis=0
        )
        weight = jnp.where(freq == 0, 1.0, 2.0).astype(jnp.float32) / (2.0 * length)
        term = lax.dot_general(
            power * weight[None, :],
            cosine,
            (((1,), (1,)), ((), ())),
            precision=lax.Precision.HIGHEST,
        )
        return (corr + term, None)

    corr, _ = lax.scan(add_block, jnp.zeros((count, length), jnp.float32), starts)
    parity = jnp.where(frame % 2 == 0, 1.0, -1.0).astype(jnp.float32)
    highest = jnp.dot(parity, series, precision=lax.Precision.HIGHEST)
    power_top = jnp.sum((highest * highest).reshape(3, count), axis=0)
    corr = corr + power_top[:, None] * parity[None, :] / (2.0 * length)
    counts = (length - frame).astype(jnp.float32)
    return (jnp.transpose(head + tail) - 2.0 * corr) / counts[None, :]


def add_carry(earlier, later):
    return earlier + later


def per_device(displacements):
    local_frames, _, atom_count = displacements.shape
    groups = lax.axis_size("frames")
    atom_total = atom_count * lax.axis_size("atoms")
    summed = lax.psum(jnp.sum(displacements, axis=2), "atoms")
    centred = displacements - (summed / atom_total)[:, :, None]
    partial_value = jnp.cumsum(centred, axis=0)
    earlier = carried_in(partial_value[-1], "frames", add_carry, jnp.zeros_like(partial_value[-1]))
    positions = (partial_value + earlier[None]).reshape(
        local_frames, 3, groups, atom_count // groups
    )
    return lag_table(lax.all_to_all(positions, "frames", split_axis=2, concat_axis=0, tiled=True))


def tables():
    points = 2 * BLOCK
    index = np.arange(BLOCK)
    angle = 2.0 * np.pi * (np.outer(index, index) % points) / points
    forward = np.zeros((points + 16, BLOCK))
    forward[:BLOCK] = np.cos(angle)
    forward[BLOCK:points] = -np.sin(angle)
    forward[points] = 1.0 - 2.0 * (index % 2)
    high = forward.astype(ml_dtypes.bfloat16)
    low = (forward - high.astype(np.float64)).astype(ml_dtypes.bfloat16)
    weight = np.where(index == 0, 1.0, 2.0)[None, :] / points
    inverse = np.concatenate([np.cos(angle) * weight, -np.sin(angle) * weight], axis=1)
    row, col = index[:, None], index[None, :]
    sums = np.stack([col <= row, col >= row, col <= BLOCK - 1 - row])
    return (
        np.stack([high, low]),
        sums.astype(ml_dtypes.bfloat16),
        (-2.0 * inverse).astype(np.float32),
    )


def split(value, terms):
    parts = []
    for _ in range(terms - 1):
        part = value.astype(jnp.bfloat16)
        parts.append(part)
        value = value - part.astype(jnp.float32)
    return parts + [value.astype(jnp.bfloat16)]


def mm(a, b):
    return jnp.dot(a, b, preferred_element_type=jnp.float32)


def kernel(
    groups, atom_total, x, forward, sums, inverse, out,
    xv, recv, mine, sibling, total, msgs, fv, sv, iv, drift, spectrum, acc_re, acc_im, acc_top, squares,
    load_sem, const_sem, own_sem, send_sem, recv_sem, pair_send, pair_recv, msg_send, msg_recv,
):
    me, core = lax.axis_index("frames"), lax.axis_index("atoms")
    frames = x.shape[1]
    width = recv.shape[2]
    blocks = recv.shape[1] // BLOCK
    tiles = x.shape[2] // LANES

    loads = [pltpu.make_async_copy(x.at[c], xv.at[c], load_sem.at[c]) for c in range(3)]
    for load in loads:
        load.start()
    consts = [
        pltpu.make_async_copy(src, dst, const_sem.at[i])
        for i, (src, dst) in enumerate(((forward, fv), (sums, sv), (inverse, iv)))
    ]
    for const in consts:
        const.start()

    def peer_at(k):
        return lax.rem(me + k, groups)

    def own_copy(c):
        return pltpu.make_async_copy(
            x.at[c, :, pl.ds(pl.multiple_of(me * width, width), width)],
            recv.at[c, pl.ds(pl.multiple_of(me * frames, frames), frames), :],
            own_sem.at[c],
        )

    barrier = pltpu.get_barrier_semaphore()

    def greet(k, carry):
        pl.semaphore_signal(barrier, inc=1, device_id={"frames": peer_at(k)}, device_id_type=MESH)
        return carry

    pl.semaphore_signal(barrier, inc=1, device_id={"atoms": 1 - core}, device_id_type=MESH)
    lax.fori_loop(1, groups, greet, 0)
    pl.semaphore_wait(barrier, groups)

    half = groups // 2
    side = me // half
    spot = lax.rem(me, half)

    def send_half(c, far):
        start = (1 - side if far else side) * half

        def send(k, carry):
            peer = start + lax.rem(spot + k, half)
            pltpu.make_async_remote_copy(
                src_ref=x.at[c, :, pl.ds(pl.multiple_of(peer * width, width), width)],
                dst_ref=recv.at[c, pl.ds(pl.multiple_of(me * frames, frames), frames), :],
                send_sem=send_sem.at[c, int(far)],
                recv_sem=recv_sem.at[c, int(far)],
                device_id={"frames": peer},
                device_id_type=MESH,
            ).start()
            return carry

        lax.fori_loop(0 if far else 1, half, send, 0)
        if not far:
            own_copy(c).start()

    send_half(0, True)
    send_half(0, False)

    parts = []
    for c in range(3):
        loads[c].wait()
        part = xv[c, :, 0:LANES]
        for tile in range(1, tiles):
            part = part + xv[c, :, tile * LANES : (tile + 1) * LANES]
        parts.append(part)
    lanes = mine.shape[1]
    if lanes > 3 * frames:
        parts.append(jnp.zeros((lanes - 3 * frames, LANES), jnp.float32))
    mine[...] = jnp.sum(jnp.transpose(jnp.concatenate(parts, axis=0)), axis=0, keepdims=True)
    pair = pltpu.make_async_remote_copy(
        src_ref=mine,
        dst_ref=sibling,
        send_sem=pair_send,
        recv_sem=pair_recv,
        device_id={"atoms": 1 - core},
        device_id_type=MESH,
    )
    pair.start()
    pair.wait()
    total[...] = (mine[...] + sibling[...]) / atom_total

    def tell(k):
        return pltpu.make_async_remote_copy(
            src_ref=total,
            dst_ref=msgs.at[me],
            send_sem=msg_send.at[k],
            recv_sem=msg_recv.at[k],
            device_id={"frames": peer_at(k)},
            device_id_type=MESH,
        )

    def tell_start(k, carry):
        tell(k).start()
        return carry

    lax.fori_loop(1, groups, tell_start, 0)
    send_half(1, True)
    send_half(1, False)
    send_half(2, False)
    msgs[pl.ds(me, 1)] = total[...][None]

    acc_re[...] = jnp.zeros_like(acc_re)
    acc_im[...] = jnp.zeros_like(acc_im)
    acc_top[...] = jnp.zeros_like(acc_top)
    squares[...] = jnp.zeros_like(squares)
    for const in consts:
        const.wait()

    def heard(k, carry):
        source = lax.rem(me + groups - k, groups)
        pltpu.make_async_remote_copy(
            src_ref=total,
            dst_ref=msgs.at[source],
            send_sem=msg_send.at[k],
            recv_sem=msg_recv.at[k],
            device_id={"frames": source},
            device_id_type=MESH,
        ).wait()
        return carry

    lax.fori_loop(1, groups, heard, 0)

    def spread(b, carry):
        column = jnp.transpose(jnp.broadcast_to(msgs[pl.ds(b, 1)][0], (LANES, lanes)))
        for c in range(3):
            drift[c, pl.ds(pl.multiple_of(b * frames, frames), frames), :] = column[
                c * frames : (c + 1) * frames
            ]
        return carry

    lax.fori_loop(0, groups, spread, 0)

    def several(c, far):
        return recv.at[c, pl.ds(0, (half if far else half - 1) * frames), :]

    def sent(c, far):
        gone = several(c, far)
        pltpu.make_async_copy(gone, gone, send_sem.at[c, int(far)]).wait()

    def arrived(c, far):
        came = several(c, far)
        pltpu.make_async_copy(came, came, recv_sem.at[c, int(far)]).wait()

    sent(0, True)
    send_half(2, True)

    def lanes_of(value):
        return [value[:, i : i + width] for i in range(0, value.shape[1], width)]

    def transform(c, which):
        pieces = []
        for i in range(blocks // 2):
            at = pl.ds(pl.multiple_of((which * (blocks // 2) + i) * BLOCK, BLOCK), BLOCK)
            pieces.append(recv[c, at, :] - drift[c, at, :])
        high, mid, low = split(jnp.concatenate(pieces, axis=1), 3)
        running = mm(sv[0], high) + (mm(sv[0], mid) + mm(sv[0], low))
        first, second = lanes_of(running[BLOCK - 1 : BLOCK, :])
        later = jnp.full((1, 1), which, jnp.int32).astype(jnp.float32)
        sooner = 1.0 - later
        shift = jnp.concatenate([-sooner * (first + second), later * first - sooner * second], axis=1)
        positions = running + shift
        squares[which] += positions * positions
        high, low = split(positions, 2)
        spectrum[which] = mm(fv[0], high) + (mm(fv[0], low) + mm(fv[1], high))

    def spectra(at):
        return lanes_of(spectrum[0, at, :]) + lanes_of(spectrum[1, at, :])

    def component(c, carry):
        own_copy(c).wait()
        arrived(c, False)
        transform(c, side)
        arrived(c, True)
        transform(c, 1 - side)

        def rows(r, inner):
            at = pl.ds(pl.multiple_of(r * 8, 8), 8)
            re = spectra(at)
            im = spectra(pl.ds(pl.multiple_of(BLOCK + r * 8, 8), 8))
            for d in range(blocks):
                here = slice(d * width, (d + 1) * width)
                real = acc_re[at, here]
                imag = acc_im[at, here]
                for i in range(blocks - d):
                    j = i + d
                    real = real + (re[i] * re[j] + im[i] * im[j])
                    if d:
                        imag = imag + (re[i] * im[j] - im[i] * re[j])
                acc_re[at, here] = real
                if d:
                    acc_im[at, here] = imag
            return inner

        lax.fori_loop(0, BLOCK // 8, rows, 0, unroll=2)
        top = spectra(pl.ds(2 * BLOCK, 8))
        for d in range(blocks):
            here = slice(d * width, (d + 1) * width)
            value = acc_top[:, here]
            for i in range(blocks - d):
                value = value + top[i] * top[i + d]
            acc_top[:, here] = value
        return carry

    lax.fori_loop(0, 3, component, 0)

    def next_block(value):
        return jnp.concatenate([value[:, width:], jnp.zeros_like(value[:, :width])], axis=1)

    parity = (1 - 2 * (lax.broadcasted_iota(jnp.int32, (BLOCK, 1), 0) % 2)).astype(jnp.float32)
    real, imag, top = acc_re[...], acc_im[...], acc_top[0:1, :]
    cross = jnp.concatenate(
        [real + parity * next_block(real), imag + parity * next_block(imag)], axis=0
    )
    corr = jnp.dot(
        iv[...], cross, precision=lax.Precision.HIGHEST, preferred_element_type=jnp.float32
    )
    corr = corr - (top + next_block(top)) * (parity * (1.0 / BLOCK))
    parts = split(jnp.concatenate([squares[0], squares[1]], axis=1), 3)
    later = mm(sv[1], parts[0]) + (mm(sv[1], parts[1]) + mm(sv[1], parts[2]))
    parts = [jnp.concatenate(lanes_of(part)[::-1], axis=1) for part in parts]
    earlier = mm(sv[2], parts[0]) + (mm(sv[2], parts[1]) + mm(sv[2], parts[2]))
    sums_of = lanes_of(later[0:1, :])
    whole = []
    for i in range(blocks):
        value = jnp.zeros((1, width), jnp.float32)
        for j in list(range(i + 1, blocks)) + list(range(blocks - 1 - i)):
            value = value + sums_of[j]
        whole.append(value)
    result = later + earlier + jnp.concatenate(whole, axis=1) + corr
    for i, piece in enumerate(lanes_of(result)):
        out[:, i * BLOCK : (i + 1) * BLOCK] = jnp.transpose(piece)

    for c, far in ((0, False), (1, True), (1, False), (2, False), (2, True)):
        sent(c, far)


def fused(displacements):
    frames, _, atom_count = displacements.shape
    groups = lax.axis_size("frames")
    length = frames * groups
    width = atom_count // groups
    blocks = length // BLOCK
    forward, sums, inverse = tables()
    lanes = -(-3 * frames // LANES) * LANES
    f32, bf16 = jnp.float32, jnp.bfloat16
    dma = pltpu.SemaphoreType.DMA
    numerator = pl.pallas_call(
        functools.partial(kernel, groups, atom_count * lax.axis_size("atoms")),
        out_shape=jax.ShapeDtypeStruct((width, length), f32),
        in_specs=[pl.BlockSpec(memory_space=pltpu.HBM)] * 4,
        out_specs=pl.BlockSpec(memory_space=pltpu.VMEM),
        scratch_shapes=[
            pltpu.VMEM((3, frames, atom_count), f32),
            pltpu.VMEM((3, length, width), f32),
            pltpu.VMEM((1, lanes), f32),
            pltpu.VMEM((1, lanes), f32),
            pltpu.VMEM((1, lanes), f32),
            pltpu.VMEM((groups, 1, lanes), f32),
            pltpu.VMEM(forward.shape, bf16),
            pltpu.VMEM(sums.shape, bf16),
            pltpu.VMEM(inverse.shape, f32),
            pltpu.VMEM((3, length, width), f32),
            pltpu.VMEM((2, 2 * BLOCK + 16, blocks * width // 2), f32),
            pltpu.VMEM((BLOCK, blocks * width), f32),
            pltpu.VMEM((BLOCK, blocks * width), f32),
            pltpu.VMEM((8, blocks * width), f32),
            pltpu.VMEM((2, BLOCK, blocks * width // 2), f32),
            dma((3,)), dma((3,)), dma((3,)), dma((3, 2)), dma((3, 2)),
            dma, dma, dma((groups,)), dma((groups,)),
        ],
        compiler_params=pltpu.CompilerParams(
            collective_id=0, has_side_effects=True, vmem_limit_bytes=40 * 1024 * 1024
        ),
    )(jnp.transpose(displacements, (1, 0, 2)), jnp.asarray(forward), jnp.asarray(sums), jnp.asarray(inverse))
    counts = (length - jnp.arange(length)).astype(f32)
    return numerator / counts[None, :]


def fits(mesh, shape):
    groups, pairs = mesh.shape["frames"], mesh.shape["atoms"]
    length, _, atoms = shape
    if pairs != 2 or groups % 2 or atoms != pairs * groups * LANES or length != 4 * BLOCK:
        return False
    return length // groups % 8 == 0


def solution(mesh):
    def run(displacements):
        return jax.shard_map(
            fused if fits(mesh, displacements.shape) else per_device,
            mesh=mesh,
            in_specs=(P("frames", None, "atoms"),),
            out_specs=P(("atoms", "frames"), None),
            check_vma=False,
        )(displacements)

    return run
```

```python
import functools
import math

import jax
import jax.numpy as jnp
import ml_dtypes
import numpy as np
from jax import lax
from jax.experimental import pallas as pl
from jax.experimental.pallas import tpu as pltpu
from jax.sharding import PartitionSpec as P


BLOCK = 256
LANES = 128
MESH = pl.DeviceIdType.MESH


def carried_in(array, axis, combine, identity):
    count, index = (lax.axis_size(axis), lax.axis_index(axis))
    everything = lax.all_gather(array, axis)
    start = jnp.broadcast_to(jnp.asarray(identity, array.dtype), array.shape)

    def hop(k, before):
        reached = k < index
        new = combine(before, everything[k])
        return jnp.where(reached, new, before)

    return lax.fori_loop(0, count, hop, start)


def lag_table(positions):
    length = positions.shape[0]
    count = positions.shape[3]
    series = positions.reshape(length, 3 * count)
    squares = jnp.sum(positions * positions, axis=(1, 2))
    zero_row = jnp.zeros((1, count), jnp.float32)
    running = jnp.concatenate([zero_row, jnp.cumsum(squares, axis=0)], axis=0)
    head = running[length][None, :] - running[:length]
    tail = jnp.flip(running[1:], 0)
    block = min(256, length)
    frame = jnp.arange(length, dtype=jnp.int32)
    starts = jnp.arange(0, length, block, dtype=jnp.int32)

    def add_block(corr, start):
        freq = start + jnp.arange(block, dtype=jnp.int32)
        phase = frame[:, None] * freq[None, :] % (2 * length)
        angle = phase.astype(jnp.float32) * (math.pi / length)
        cosine = jnp.cos(angle)
        sine = jnp.sin(angle)
        real_part = lax.dot_general(
            series, cosine, (((0,), (0,)), ((), ())), precision=lax.Precision.HIGHEST
        )
        imag_part = lax.dot_general(
            series, sine, (((0,), (0,)), ((), ())), precision=lax.Precision.HIGHEST
        )
        power = jnp.sum(
            (real_part * real_part + imag_part * imag_part).reshape(3, count, block), axis=0
        )
        weight = jnp.where(freq == 0, 1.0, 2.0).astype(jnp.float32) / (2.0 * length)
        term = lax.dot_general(
            power * weight[None, :],
            cosine,
            (((1,), (1,)), ((), ())),
            precision=lax.Precision.HIGHEST,
        )
        return (corr + term, None)

    corr, _ = lax.scan(add_block, jnp.zeros((count, length), jnp.float32), starts)
    parity = jnp.where(frame % 2 == 0, 1.0, -1.0).astype(jnp.float32)
    highest = jnp.dot(parity, series, precision=lax.Precision.HIGHEST)
    power_top = jnp.sum((highest * highest).reshape(3, count), axis=0)
    corr = corr + power_top[:, None] * parity[None, :] / (2.0 * length)
    counts = (length - frame).astype(jnp.float32)
    return (jnp.transpose(head + tail) - 2.0 * corr) / counts[None, :]


def add_carry(earlier, later):
    return earlier + later


def per_device(displacements):
    local_frames, _, atom_count = displacements.shape
    groups = lax.axis_size("frames")
    atom_total = atom_count * lax.axis_size("atoms")
    summed = lax.psum(jnp.sum(displacements, axis=2), "atoms")
    centred = displacements - (summed / atom_total)[:, :, None]
    partial_value = jnp.cumsum(centred, axis=0)
    earlier = carried_in(partial_value[-1], "frames", add_carry, jnp.zeros_like(partial_value[-1]))
    positions = (partial_value + earlier[None]).reshape(
        local_frames, 3, groups, atom_count // groups
    )
    return lag_table(lax.all_to_all(positions, "frames", split_axis=2, concat_axis=0, tiled=True))


def tables():
    points = 2 * BLOCK
    index = np.arange(BLOCK)
    angle = 2.0 * np.pi * (np.outer(index, index) % points) / points
    forward = np.zeros((points + 16, BLOCK))
    forward[:BLOCK] = np.cos(angle)
    forward[BLOCK:points] = -np.sin(angle)
    forward[points] = 1.0 - 2.0 * (index % 2)
    weight = np.where(index == 0, 1.0, 2.0)[None, :] / points
    inverse = [-2.0 * np.cos(angle) * weight, 2.0 * np.sin(angle) * weight]
    row, col = index[:, None], index[None, :]
    sums = [col <= row, col >= row, col <= BLOCK - 1 - row]
    pieces = rounded(forward, 2)
    pieces += [part.astype(ml_dtypes.bfloat16) for part in sums]
    pieces += [part for pair in zip(*(rounded(half, 3) for half in inverse)) for part in pair]
    return np.concatenate(pieces, axis=0)


def rounded(values, terms):
    parts = []
    for _ in range(terms):
        part = values.astype(ml_dtypes.bfloat16)
        parts.append(part)
        values = values - part.astype(np.float64)
    return parts


def split(value, terms):
    parts = []
    for _ in range(terms - 1):
        part = value.astype(jnp.bfloat16)
        parts.append(part)
        value = value - part.astype(jnp.float32)
    return parts + [value.astype(jnp.bfloat16)]


def mm(a, b):
    return jnp.dot(a, b, preferred_element_type=jnp.float32)


def kernel(
    groups, atom_total, x, table, out,
    xv, recv, mine, sibling, total, msgs, held, drift, spectrum, acc_re, acc_im, acc_top, squares,
    load_sem, const_sem, own_sem, send_sem, recv_sem, pair_send, pair_recv, msg_send, msg_recv,
):
    me, core = lax.axis_index("frames"), lax.axis_index("atoms")
    frames = x.shape[1]
    width = recv.shape[2]
    blocks = recv.shape[1] // BLOCK
    tiles = x.shape[2] // LANES

    loads = [pltpu.make_async_copy(x.at[c], xv.at[c], load_sem.at[c]) for c in range(3)]
    for load in loads:
        load.start()
    const = pltpu.make_async_copy(table, held, const_sem)
    const.start()
    tall = 2 * BLOCK + 16

    def forward(part):
        return held[part * tall : (part + 1) * tall, :]

    def sums(which):
        start = 2 * tall + which * BLOCK
        return held[start : start + BLOCK, :]

    def inverse(part, which):
        start = 2 * tall + (3 + 2 * part + which) * BLOCK
        return held[start : start + BLOCK, :]

    def peer_at(k):
        return lax.rem(me + k, groups)

    def own_copy(c):
        return pltpu.make_async_copy(
            x.at[c, :, pl.ds(pl.multiple_of(me * width, width), width)],
            recv.at[c, pl.ds(pl.multiple_of(me * frames, frames), frames), :],
            own_sem.at[c],
        )

    barrier = pltpu.get_barrier_semaphore()

    def greet(k, carry):
        pl.semaphore_signal(barrier, inc=1, device_id={"frames": peer_at(k)}, device_id_type=MESH)
        return carry

    pl.semaphore_signal(barrier, inc=1, device_id={"atoms": 1 - core}, device_id_type=MESH)
    lax.fori_loop(1, groups, greet, 0)
    pl.semaphore_wait(barrier, groups)

    half = groups // 2
    side = me // half
    spot = lax.rem(me, half)

    def send_one(c, far, k):
        peer = (1 - side if far else side) * half + lax.rem(spot + k, half)
        pltpu.make_async_remote_copy(
            src_ref=x.at[c, :, pl.ds(pl.multiple_of(peer * width, width), width)],
            dst_ref=recv.at[c, pl.ds(pl.multiple_of(me * frames, frames), frames), :],
            send_sem=send_sem.at[c, int(far)],
            recv_sem=recv_sem.at[c, int(far)],
            device_id={"frames": peer},
            device_id_type=MESH,
        ).start()

    def send_component(c):
        def send(k, carry):
            send_one(c, True, k)
            send_one(c, False, k)
            return carry

        send_one(c, True, 0)
        lax.fori_loop(1, half, send, 0)
        own_copy(c).start()

    send_component(0)

    parts = []
    for c in range(3):
        loads[c].wait()
        part = xv[c, :, 0:LANES]
        for tile in range(1, tiles):
            part = part + xv[c, :, tile * LANES : (tile + 1) * LANES]
        parts.append(part)
    lanes = mine.shape[1]
    if lanes > 3 * frames:
        parts.append(jnp.zeros((lanes - 3 * frames, LANES), jnp.float32))
    mine[...] = jnp.sum(jnp.transpose(jnp.concatenate(parts, axis=0)), axis=0, keepdims=True)
    pair = pltpu.make_async_remote_copy(
        src_ref=mine,
        dst_ref=sibling,
        send_sem=pair_send,
        recv_sem=pair_recv,
        device_id={"atoms": 1 - core},
        device_id_type=MESH,
    )
    pair.start()
    pair.wait()
    total[...] = (mine[...] + sibling[...]) / atom_total

    def tell(k):
        return pltpu.make_async_remote_copy(
            src_ref=total,
            dst_ref=msgs.at[me],
            send_sem=msg_send.at[k],
            recv_sem=msg_recv.at[k],
            device_id={"frames": peer_at(k)},
            device_id_type=MESH,
        )

    def tell_start(k, carry):
        tell(k).start()
        return carry

    lax.fori_loop(1, groups, tell_start, 0)
    send_component(1)
    msgs[pl.ds(me, 1)] = total[...][None]

    acc_re[...] = jnp.zeros_like(acc_re)
    acc_im[...] = jnp.zeros_like(acc_im)
    acc_top[...] = jnp.zeros_like(acc_top)
    squares[...] = jnp.zeros_like(squares)
    const.wait()

    def heard(k, carry):
        source = lax.rem(me + groups - k, groups)
        pltpu.make_async_remote_copy(
            src_ref=total,
            dst_ref=msgs.at[source],
            send_sem=msg_send.at[k],
            recv_sem=msg_recv.at[k],
            device_id={"frames": source},
            device_id_type=MESH,
        ).wait()
        return carry

    lax.fori_loop(1, groups, heard, 0)

    def spread(b, carry):
        column = jnp.transpose(jnp.broadcast_to(msgs[pl.ds(b, 1)][0], (LANES, lanes)))
        for c in range(3):
            drift[c, pl.ds(pl.multiple_of(b * frames, frames), frames), :] = column[
                c * frames : (c + 1) * frames
            ]
        return carry

    lax.fori_loop(0, groups, spread, 0)

    def several(c, far):
        return recv.at[c, pl.ds(0, (half if far else half - 1) * frames), :]

    def sent(c, far):
        gone = several(c, far)
        pltpu.make_async_copy(gone, gone, send_sem.at[c, int(far)]).wait()

    def arrived(c, far):
        came = several(c, far)
        pltpu.make_async_copy(came, came, recv_sem.at[c, int(far)]).wait()

    sent(0, True)
    send_component(2)

    def lanes_of(value):
        return [value[:, i : i + width] for i in range(0, value.shape[1], width)]

    def transform(c, which):
        pieces = []
        for i in range(blocks // 2):
            at = pl.ds(pl.multiple_of((which * (blocks // 2) + i) * BLOCK, BLOCK), BLOCK)
            pieces.append(recv[c, at, :] - drift[c, at, :])
        high, mid, low = split(jnp.concatenate(pieces, axis=1), 3)
        running = mm(sums(0), high) + (mm(sums(0), mid) + mm(sums(0), low))
        first, second = lanes_of(running[BLOCK - 1 : BLOCK, :])
        later = jnp.full((1, 1), which, jnp.int32).astype(jnp.float32)
        sooner = 1.0 - later
        shift = jnp.concatenate([-sooner * (first + second), later * first - sooner * second], axis=1)
        positions = running + shift
        squares[which] += positions * positions
        high, low = split(positions, 2)
        spectrum[which] = mm(forward(0), high) + (mm(forward(0), low) + mm(forward(1), high))

    def spectra(at):
        return lanes_of(spectrum[0, at, :]) + lanes_of(spectrum[1, at, :])

    def component(c, carry):
        own_copy(c).wait()
        arrived(c, False)
        transform(c, side)
        arrived(c, True)
        transform(c, 1 - side)

        def rows(r, inner):
            at = pl.ds(pl.multiple_of(r * 8, 8), 8)
            re = spectra(at)
            im = spectra(pl.ds(pl.multiple_of(BLOCK + r * 8, 8), 8))
            for d in range(blocks):
                here = slice(d * width, (d + 1) * width)
                real = acc_re[at, here]
                imag = acc_im[at, here]
                for i in range(blocks - d):
                    j = i + d
                    real = real + (re[i] * re[j] + im[i] * im[j])
                    if d:
                        imag = imag + (re[i] * im[j] - im[i] * re[j])
                acc_re[at, here] = real
                if d:
                    acc_im[at, here] = imag
            return inner

        lax.fori_loop(0, BLOCK // 8, rows, 0, unroll=2)
        top = spectra(pl.ds(2 * BLOCK, 8))
        for d in range(blocks):
            here = slice(d * width, (d + 1) * width)
            value = acc_top[:, here]
            for i in range(blocks - d):
                value = value + top[i] * top[i + d]
            acc_top[:, here] = value
        return carry

    lax.fori_loop(0, 3, component, 0)

    def next_block(value):
        return jnp.concatenate([value[:, width:], jnp.zeros_like(value[:, :width])], axis=1)

    parity = (1 - 2 * (lax.broadcasted_iota(jnp.int32, (BLOCK, 1), 0) % 2)).astype(jnp.float32)
    real, imag, top = acc_re[...], acc_im[...], acc_top[0:1, :]
    cross = [split(real + parity * next_block(real), 3), split(imag + parity * next_block(imag), 3)]
    corr = jnp.zeros_like(real)
    for a, b in ((2, 0), (0, 2), (1, 1), (1, 0), (0, 1), (0, 0)):
        corr = corr + (mm(inverse(a, 0), cross[0][b]) + mm(inverse(a, 1), cross[1][b]))
    corr = corr - (top + next_block(top)) * (parity * (1.0 / BLOCK))
    parts = split(jnp.concatenate([squares[0], squares[1]], axis=1), 3)
    later = mm(sums(1), parts[0]) + (mm(sums(1), parts[1]) + mm(sums(1), parts[2]))
    parts = [jnp.concatenate(lanes_of(part)[::-1], axis=1) for part in parts]
    earlier = mm(sums(2), parts[0]) + (mm(sums(2), parts[1]) + mm(sums(2), parts[2]))
    sums_of = lanes_of(later[0:1, :])
    whole = []
    for i in range(blocks):
        value = jnp.zeros((1, width), jnp.float32)
        for j in list(range(i + 1, blocks)) + list(range(blocks - 1 - i)):
            value = value + sums_of[j]
        whole.append(value)
    result = later + earlier + jnp.concatenate(whole, axis=1) + corr
    for i, piece in enumerate(lanes_of(result)):
        out[:, i * BLOCK : (i + 1) * BLOCK] = jnp.transpose(piece)

    for c, far in ((0, False), (1, True), (1, False), (2, False), (2, True)):
        sent(c, far)


def fused(displacements):
    frames, _, atom_count = displacements.shape
    groups = lax.axis_size("frames")
    length = frames * groups
    width = atom_count // groups
    blocks = length // BLOCK
    table = tables()
    lanes = -(-3 * frames // LANES) * LANES
    f32, bf16 = jnp.float32, jnp.bfloat16
    dma = pltpu.SemaphoreType.DMA
    numerator = pl.pallas_call(
        functools.partial(kernel, groups, atom_count * lax.axis_size("atoms")),
        out_shape=jax.ShapeDtypeStruct((width, length), f32),
        in_specs=[pl.BlockSpec(memory_space=pltpu.HBM)] * 2,
        out_specs=pl.BlockSpec(memory_space=pltpu.VMEM),
        scratch_shapes=[
            pltpu.VMEM((3, frames, atom_count), f32),
            pltpu.VMEM((3, length, width), f32),
            pltpu.VMEM((1, lanes), f32),
            pltpu.VMEM((1, lanes), f32),
            pltpu.VMEM((1, lanes), f32),
            pltpu.VMEM((groups, 1, lanes), f32),
            pltpu.VMEM(table.shape, bf16),
            pltpu.VMEM((3, length, width), f32),
            pltpu.VMEM((2, 2 * BLOCK + 16, blocks * width // 2), f32),
            pltpu.VMEM((BLOCK, blocks * width), f32),
            pltpu.VMEM((BLOCK, blocks * width), f32),
            pltpu.VMEM((8, blocks * width), f32),
            pltpu.VMEM((2, BLOCK, blocks * width // 2), f32),
            dma((3,)), dma, dma((3,)), dma((3, 2)), dma((3, 2)),
            dma, dma, dma((groups,)), dma((groups,)),
        ],
        compiler_params=pltpu.CompilerParams(
            collective_id=0, has_side_effects=True, vmem_limit_bytes=62_200_000
        ),
    )(jnp.transpose(displacements, (1, 0, 2)), jnp.asarray(table))
    counts = (length - jnp.arange(length)).astype(f32)
    return numerator / counts[None, :]


def fits(mesh, shape):
    groups, pairs = mesh.shape["frames"], mesh.shape["atoms"]
    length, _, atoms = shape
    if pairs != 2 or groups % 2 or atoms != pairs * groups * LANES or length != 4 * BLOCK:
        return False
    return length // groups % 8 == 0


def solution(mesh):
    def run(displacements):
        return jax.shard_map(
            fused if fits(mesh, displacements.shape) else per_device,
            mesh=mesh,
            in_specs=(P("frames", None, "atoms"),),
            out_specs=P(("atoms", "frames"), None),
            check_vma=False,
        )(displacements)

    return run
```

```python
import functools
import math

import jax
import jax.numpy as jnp
import ml_dtypes
import numpy as np
from jax import lax
from jax.experimental import pallas as pl
from jax.experimental.pallas import tpu as pltpu
from jax.sharding import PartitionSpec as P


BLOCK = 256
LANES = 128
MESH = pl.DeviceIdType.MESH


def carried_in(array, axis, combine, identity):
    count, index = (lax.axis_size(axis), lax.axis_index(axis))
    everything = lax.all_gather(array, axis)
    start = jnp.broadcast_to(jnp.asarray(identity, array.dtype), array.shape)

    def hop(k, before):
        reached = k < index
        new = combine(before, everything[k])
        return jnp.where(reached, new, before)

    return lax.fori_loop(0, count, hop, start)


def lag_table(positions):
    length = positions.shape[0]
    count = positions.shape[3]
    series = positions.reshape(length, 3 * count)
    squares = jnp.sum(positions * positions, axis=(1, 2))
    zero_row = jnp.zeros((1, count), jnp.float32)
    running = jnp.concatenate([zero_row, jnp.cumsum(squares, axis=0)], axis=0)
    head = running[length][None, :] - running[:length]
    tail = jnp.flip(running[1:], 0)
    block = min(256, length)
    frame = jnp.arange(length, dtype=jnp.int32)
    starts = jnp.arange(0, length, block, dtype=jnp.int32)

    def add_block(corr, start):
        freq = start + jnp.arange(block, dtype=jnp.int32)
        phase = frame[:, None] * freq[None, :] % (2 * length)
        angle = phase.astype(jnp.float32) * (math.pi / length)
        cosine = jnp.cos(angle)
        sine = jnp.sin(angle)
        real_part = lax.dot_general(
            series, cosine, (((0,), (0,)), ((), ())), precision=lax.Precision.HIGHEST
        )
        imag_part = lax.dot_general(
            series, sine, (((0,), (0,)), ((), ())), precision=lax.Precision.HIGHEST
        )
        power = jnp.sum(
            (real_part * real_part + imag_part * imag_part).reshape(3, count, block), axis=0
        )
        weight = jnp.where(freq == 0, 1.0, 2.0).astype(jnp.float32) / (2.0 * length)
        term = lax.dot_general(
            power * weight[None, :],
            cosine,
            (((1,), (1,)), ((), ())),
            precision=lax.Precision.HIGHEST,
        )
        return (corr + term, None)

    corr, _ = lax.scan(add_block, jnp.zeros((count, length), jnp.float32), starts)
    parity = jnp.where(frame % 2 == 0, 1.0, -1.0).astype(jnp.float32)
    highest = jnp.dot(parity, series, precision=lax.Precision.HIGHEST)
    power_top = jnp.sum((highest * highest).reshape(3, count), axis=0)
    corr = corr + power_top[:, None] * parity[None, :] / (2.0 * length)
    counts = (length - frame).astype(jnp.float32)
    return (jnp.transpose(head + tail) - 2.0 * corr) / counts[None, :]


def add_carry(earlier, later):
    return earlier + later


def per_device(displacements):
    local_frames, _, atom_count = displacements.shape
    groups = lax.axis_size("frames")
    atom_total = atom_count * lax.axis_size("atoms")
    summed = lax.psum(jnp.sum(displacements, axis=2), "atoms")
    centred = displacements - (summed / atom_total)[:, :, None]
    partial_value = jnp.cumsum(centred, axis=0)
    earlier = carried_in(partial_value[-1], "frames", add_carry, jnp.zeros_like(partial_value[-1]))
    positions = (partial_value + earlier[None]).reshape(
        local_frames, 3, groups, atom_count // groups
    )
    return lag_table(lax.all_to_all(positions, "frames", split_axis=2, concat_axis=0, tiled=True))


def tables():
    points = 2 * BLOCK
    index = np.arange(BLOCK)
    angle = 2.0 * np.pi * (np.outer(index, index) % points) / points
    forward = np.zeros((points + 16, BLOCK))
    forward[:BLOCK] = np.cos(angle)
    forward[BLOCK:points] = -np.sin(angle)
    forward[points] = 1.0 - 2.0 * (index % 2)
    weight = np.where(index == 0, 1.0, 2.0)[None, :] / points
    inverse = [-2.0 * np.cos(angle) * weight, 2.0 * np.sin(angle) * weight]
    row, col = index[:, None], index[None, :]
    sums = [col <= row, col >= row, col <= BLOCK - 1 - row]
    pieces = rounded(forward, 2)
    pieces += [part.astype(ml_dtypes.bfloat16) for part in sums]
    pieces += [part for pair in zip(*(rounded(half, 2) for half in inverse)) for part in pair]
    return np.concatenate(pieces, axis=0)


def rounded(values, terms):
    parts = []
    for _ in range(terms):
        part = values.astype(ml_dtypes.bfloat16)
        parts.append(part)
        values = values - part.astype(np.float64)
    return parts


def split(value, terms):
    parts = []
    for _ in range(terms - 1):
        part = value.astype(jnp.bfloat16)
        parts.append(part)
        value = value - part.astype(jnp.float32)
    return parts + [value.astype(jnp.bfloat16)]


def mm(a, b):
    return jnp.dot(a, b, preferred_element_type=jnp.float32)


def kernel(
    groups, atom_total, x, table, out,
    xv, recv, mine, sibling, total, msgs, held, drift, spectrum, acc_re, acc_im, acc_top, squares,
    load_sem, const_sem, own_sem, send_sem, recv_sem, pair_send, pair_recv, msg_send, msg_recv,
):
    me, core = lax.axis_index("frames"), lax.axis_index("atoms")
    frames = x.shape[1]
    width = recv.shape[2]
    blocks = recv.shape[1] // BLOCK
    tiles = x.shape[2] // LANES

    loads = [pltpu.make_async_copy(x.at[c], xv.at[c], load_sem.at[c]) for c in range(3)]
    for load in loads:
        load.start()
    const = pltpu.make_async_copy(table, held, const_sem)
    const.start()
    tall = 2 * BLOCK + 16

    def forward(part):
        return held[part * tall : (part + 1) * tall, :]

    def sums(which):
        start = 2 * tall + which * BLOCK
        return held[start : start + BLOCK, :]

    def inverse(part, which):
        start = 2 * tall + (3 + 2 * part + which) * BLOCK
        return held[start : start + BLOCK, :]

    def peer_at(k):
        return lax.rem(me + k, groups)

    def own_copy(c):
        return pltpu.make_async_copy(
            x.at[c, :, pl.ds(pl.multiple_of(me * width, width), width)],
            recv.at[c, pl.ds(pl.multiple_of(me * frames, frames), frames), :],
            own_sem.at[c],
        )

    barrier = pltpu.get_barrier_semaphore()

    def greet(k, carry):
        pl.semaphore_signal(barrier, inc=1, device_id={"frames": peer_at(k)}, device_id_type=MESH)
        return carry

    pl.semaphore_signal(barrier, inc=1, device_id={"atoms": 1 - core}, device_id_type=MESH)
    lax.fori_loop(1, groups, greet, 0)
    pl.semaphore_wait(barrier, groups)

    half = groups // 2
    side = me // half
    spot = lax.rem(me, half)

    def send_one(c, far, k):
        peer = (1 - side if far else side) * half + lax.rem(spot + k, half)
        pltpu.make_async_remote_copy(
            src_ref=x.at[c, :, pl.ds(pl.multiple_of(peer * width, width), width)],
            dst_ref=recv.at[c, pl.ds(pl.multiple_of(me * frames, frames), frames), :],
            send_sem=send_sem.at[c, int(far)],
            recv_sem=recv_sem.at[c, int(far)],
            device_id={"frames": peer},
            device_id_type=MESH,
        ).start()

    def send_component(c):
        def send(k, carry):
            send_one(c, True, k)
            send_one(c, False, k)
            return carry

        send_one(c, True, 0)
        lax.fori_loop(1, half, send, 0)
        own_copy(c).start()

    send_component(0)

    parts = []
    for c in range(3):
        loads[c].wait()
        part = xv[c, :, 0:LANES]
        for tile in range(1, tiles):
            part = part + xv[c, :, tile * LANES : (tile + 1) * LANES]
        parts.append(part)
    lanes = mine.shape[1]
    if lanes > 3 * frames:
        parts.append(jnp.zeros((lanes - 3 * frames, LANES), jnp.float32))
    mine[...] = jnp.sum(jnp.transpose(jnp.concatenate(parts, axis=0)), axis=0, keepdims=True)
    pair = pltpu.make_async_remote_copy(
        src_ref=mine,
        dst_ref=sibling,
        send_sem=pair_send,
        recv_sem=pair_recv,
        device_id={"atoms": 1 - core},
        device_id_type=MESH,
    )
    pair.start()
    pair.wait()
    total[...] = (mine[...] + sibling[...]) / atom_total

    def tell(k):
        return pltpu.make_async_remote_copy(
            src_ref=total,
            dst_ref=msgs.at[me],
            send_sem=msg_send.at[k],
            recv_sem=msg_recv.at[k],
            device_id={"frames": peer_at(k)},
            device_id_type=MESH,
        )

    def tell_start(k, carry):
        tell(k).start()
        return carry

    lax.fori_loop(1, groups, tell_start, 0)
    send_component(1)
    msgs[pl.ds(me, 1)] = total[...][None]

    acc_re[...] = jnp.zeros_like(acc_re)
    acc_im[...] = jnp.zeros_like(acc_im)
    acc_top[...] = jnp.zeros_like(acc_top)
    squares[...] = jnp.zeros_like(squares)
    const.wait()

    def heard(k, carry):
        source = lax.rem(me + groups - k, groups)
        pltpu.make_async_remote_copy(
            src_ref=total,
            dst_ref=msgs.at[source],
            send_sem=msg_send.at[k],
            recv_sem=msg_recv.at[k],
            device_id={"frames": source},
            device_id_type=MESH,
        ).wait()
        return carry

    lax.fori_loop(1, groups, heard, 0)

    def spread(b, carry):
        column = jnp.transpose(jnp.broadcast_to(msgs[pl.ds(b, 1)][0], (LANES, lanes)))
        for c in range(3):
            drift[c, pl.ds(pl.multiple_of(b * frames, frames), frames), :] = column[
                c * frames : (c + 1) * frames
            ]
        return carry

    lax.fori_loop(0, groups, spread, 0)

    def several(c, far):
        return recv.at[c, pl.ds(0, (half if far else half - 1) * frames), :]

    def sent(c, far):
        gone = several(c, far)
        pltpu.make_async_copy(gone, gone, send_sem.at[c, int(far)]).wait()

    def arrived(c, far):
        came = several(c, far)
        pltpu.make_async_copy(came, came, recv_sem.at[c, int(far)]).wait()

    sent(0, True)
    send_component(2)

    def lanes_of(value):
        return [value[:, i : i + width] for i in range(0, value.shape[1], width)]

    def transform(c, which):
        pieces = []
        for i in range(blocks // 2):
            at = pl.ds(pl.multiple_of((which * (blocks // 2) + i) * BLOCK, BLOCK), BLOCK)
            pieces.append(recv[c, at, :] - drift[c, at, :])
        high, low = split(jnp.concatenate(pieces, axis=1), 2)
        running = mm(sums(0), high) + mm(sums(0), low)
        first, second = lanes_of(running[BLOCK - 1 : BLOCK, :])
        later = jnp.full((1, 1), which, jnp.int32).astype(jnp.float32)
        sooner = 1.0 - later
        shift = jnp.concatenate([-sooner * (first + second), later * first - sooner * second], axis=1)
        positions = running + shift
        squares[which] += positions * positions
        high, low = split(positions, 2)
        spectrum[which] = mm(forward(0), high) + (mm(forward(0), low) + mm(forward(1), high))

    def spectra(at):
        return lanes_of(spectrum[0, at, :]) + lanes_of(spectrum[1, at, :])

    def component(c, carry):
        own_copy(c).wait()
        arrived(c, False)
        transform(c, side)
        arrived(c, True)
        transform(c, 1 - side)

        def rows(r, inner):
            at = pl.ds(pl.multiple_of(r * 8, 8), 8)
            re = spectra(at)
            im = spectra(pl.ds(pl.multiple_of(BLOCK + r * 8, 8), 8))
            for d in range(blocks):
                here = slice(d * width, (d + 1) * width)
                real = acc_re[at, here]
                imag = acc_im[at, here]
                for i in range(blocks - d):
                    j = i + d
                    real = real + (re[i] * re[j] + im[i] * im[j])
                    if d:
                        imag = imag + (re[i] * im[j] - im[i] * re[j])
                acc_re[at, here] = real
                if d:
                    acc_im[at, here] = imag
            return inner

        lax.fori_loop(0, BLOCK // 8, rows, 0, unroll=4)
        top = spectra(pl.ds(2 * BLOCK, 8))
        for d in range(blocks):
            here = slice(d * width, (d + 1) * width)
            value = acc_top[:, here]
            for i in range(blocks - d):
                value = value + top[i] * top[i + d]
            acc_top[:, here] = value
        return carry

    lax.fori_loop(0, 3, component, 0)

    def next_block(value):
        return jnp.concatenate([value[:, width:], jnp.zeros_like(value[:, :width])], axis=1)

    parity = (1 - 2 * (lax.broadcasted_iota(jnp.int32, (BLOCK, 1), 0) % 2)).astype(jnp.float32)
    real, imag, top = acc_re[...], acc_im[...], acc_top[0:1, :]
    cross = [split(real + parity * next_block(real), 2), split(imag + parity * next_block(imag), 2)]
    corr = jnp.zeros_like(real)
    for a, b in ((1, 0), (0, 1), (0, 0)):
        corr = corr + (mm(inverse(a, 0), cross[0][b]) + mm(inverse(a, 1), cross[1][b]))
    corr = corr - (top + next_block(top)) * (parity * (1.0 / BLOCK))
    parts = split(jnp.concatenate([squares[0], squares[1]], axis=1), 2)
    later = mm(sums(1), parts[0]) + mm(sums(1), parts[1])
    parts = [jnp.concatenate(lanes_of(part)[::-1], axis=1) for part in parts]
    earlier = mm(sums(2), parts[0]) + mm(sums(2), parts[1])
    sums_of = lanes_of(later[0:1, :])
    whole = []
    for i in range(blocks):
        value = jnp.zeros((1, width), jnp.float32)
        for j in list(range(i + 1, blocks)) + list(range(blocks - 1 - i)):
            value = value + sums_of[j]
        whole.append(value)
    result = later + earlier + jnp.concatenate(whole, axis=1) + corr
    for i, piece in enumerate(lanes_of(result)):
        lag = i * BLOCK + lax.broadcasted_iota(jnp.int32, (BLOCK, 1), 0)
        pairs = (blocks * BLOCK - lag).astype(jnp.float32)
        out[:, i * BLOCK : (i + 1) * BLOCK] = jnp.transpose(piece / pairs)

    for c, far in ((0, False), (1, True), (1, False), (2, False), (2, True)):
        sent(c, far)


def fused(displacements):
    frames, _, atom_count = displacements.shape
    groups = lax.axis_size("frames")
    length = frames * groups
    width = atom_count // groups
    blocks = length // BLOCK
    table = tables()
    lanes = -(-3 * frames // LANES) * LANES
    f32, bf16 = jnp.float32, jnp.bfloat16
    dma = pltpu.SemaphoreType.DMA
    return pl.pallas_call(
        functools.partial(kernel, groups, atom_count * lax.axis_size("atoms")),
        out_shape=jax.ShapeDtypeStruct((width, length), f32),
        in_specs=[pl.BlockSpec(memory_space=pltpu.HBM)] * 2,
        out_specs=pl.BlockSpec(memory_space=pltpu.VMEM),
        scratch_shapes=[
            pltpu.VMEM((3, frames, atom_count), f32),
            pltpu.VMEM((3, length, width), f32),
            pltpu.VMEM((1, lanes), f32),
            pltpu.VMEM((1, lanes), f32),
            pltpu.VMEM((1, lanes), f32),
            pltpu.VMEM((groups, 1, lanes), f32),
            pltpu.VMEM(table.shape, bf16),
            pltpu.VMEM((3, length, width), f32),
            pltpu.VMEM((2, 2 * BLOCK + 16, blocks * width // 2), f32),
            pltpu.VMEM((BLOCK, blocks * width), f32),
            pltpu.VMEM((BLOCK, blocks * width), f32),
            pltpu.VMEM((8, blocks * width), f32),
            pltpu.VMEM((2, BLOCK, blocks * width // 2), f32),
            dma((3,)), dma, dma((3,)), dma((3, 2)), dma((3, 2)),
            dma, dma, dma((groups,)), dma((groups,)),
        ],
        compiler_params=pltpu.CompilerParams(
            collective_id=0, has_side_effects=True, vmem_limit_bytes=60 * 1024 * 1024
        ),
    )(jnp.transpose(displacements, (1, 0, 2)), jnp.asarray(table))


def fits(mesh, shape):
    groups, pairs = mesh.shape["frames"], mesh.shape["atoms"]
    length, _, atoms = shape
    if pairs != 2 or groups % 2 or atoms != pairs * groups * LANES or length != 4 * BLOCK:
        return False
    return length // groups % 8 == 0


def solution(mesh):
    def run(displacements):
        return jax.shard_map(
            fused if fits(mesh, displacements.shape) else per_device,
            mesh=mesh,
            in_specs=(P("frames", None, "atoms"),),
            out_specs=P(("atoms", "frames"), None),
            check_vma=False,
        )(displacements)

    return run
```

```python
import functools
import math

import jax
import jax.numpy as jnp
import ml_dtypes
import numpy as np
from jax import lax
from jax.experimental import pallas as pl
from jax.experimental.pallas import tpu as pltpu
from jax.sharding import PartitionSpec as P


BLOCK = 256
LANES = 128
PIECES = 8
MESH = pl.DeviceIdType.MESH


def carried_in(array, axis, combine, identity):
    count, index = (lax.axis_size(axis), lax.axis_index(axis))
    everything = lax.all_gather(array, axis)
    start = jnp.broadcast_to(jnp.asarray(identity, array.dtype), array.shape)

    def hop(k, before):
        reached = k < index
        new = combine(before, everything[k])
        return jnp.where(reached, new, before)

    return lax.fori_loop(0, count, hop, start)


def lag_table(positions):
    length = positions.shape[0]
    count = positions.shape[3]
    series = positions.reshape(length, 3 * count)
    squares = jnp.sum(positions * positions, axis=(1, 2))
    zero_row = jnp.zeros((1, count), jnp.float32)
    running = jnp.concatenate([zero_row, jnp.cumsum(squares, axis=0)], axis=0)
    head = running[length][None, :] - running[:length]
    tail = jnp.flip(running[1:], 0)
    block = min(256, length)
    frame = jnp.arange(length, dtype=jnp.int32)
    starts = jnp.arange(0, length, block, dtype=jnp.int32)

    def add_block(corr, start):
        freq = start + jnp.arange(block, dtype=jnp.int32)
        phase = frame[:, None] * freq[None, :] % (2 * length)
        angle = phase.astype(jnp.float32) * (math.pi / length)
        cosine = jnp.cos(angle)
        sine = jnp.sin(angle)
        real_part = lax.dot_general(
            series, cosine, (((0,), (0,)), ((), ())), precision=lax.Precision.HIGHEST
        )
        imag_part = lax.dot_general(
            series, sine, (((0,), (0,)), ((), ())), precision=lax.Precision.HIGHEST
        )
        power = jnp.sum(
            (real_part * real_part + imag_part * imag_part).reshape(3, count, block), axis=0
        )
        weight = jnp.where(freq == 0, 1.0, 2.0).astype(jnp.float32) / (2.0 * length)
        term = lax.dot_general(
            power * weight[None, :],
            cosine,
            (((1,), (1,)), ((), ())),
            precision=lax.Precision.HIGHEST,
        )
        return (corr + term, None)

    corr, _ = lax.scan(add_block, jnp.zeros((count, length), jnp.float32), starts)
    parity = jnp.where(frame % 2 == 0, 1.0, -1.0).astype(jnp.float32)
    highest = jnp.dot(parity, series, precision=lax.Precision.HIGHEST)
    power_top = jnp.sum((highest * highest).reshape(3, count), axis=0)
    corr = corr + power_top[:, None] * parity[None, :] / (2.0 * length)
    counts = (length - frame).astype(jnp.float32)
    return (jnp.transpose(head + tail) - 2.0 * corr) / counts[None, :]


def add_carry(earlier, later):
    return earlier + later


def per_device(displacements):
    local_frames, _, atom_count = displacements.shape
    groups = lax.axis_size("frames")
    atom_total = atom_count * lax.axis_size("atoms")
    summed = lax.psum(jnp.sum(displacements, axis=2), "atoms")
    centred = displacements - (summed / atom_total)[:, :, None]
    partial_value = jnp.cumsum(centred, axis=0)
    earlier = carried_in(partial_value[-1], "frames", add_carry, jnp.zeros_like(partial_value[-1]))
    positions = (partial_value + earlier[None]).reshape(
        local_frames, 3, groups, atom_count // groups
    )
    return lag_table(lax.all_to_all(positions, "frames", split_axis=2, concat_axis=0, tiled=True))


def tables():
    points = 2 * BLOCK
    index = np.arange(BLOCK)
    angle = 2.0 * np.pi * (np.outer(index, index) % points) / points
    forward = np.zeros((points + 16, BLOCK))
    forward[:BLOCK] = np.cos(angle)
    forward[BLOCK:points] = -np.sin(angle)
    forward[points] = 1.0 - 2.0 * (index % 2)
    weight = np.where(index == 0, 1.0, 2.0)[None, :] / points
    inverse = [-2.0 * np.cos(angle) * weight, 2.0 * np.sin(angle) * weight]
    row, col = index[:, None], index[None, :]
    sums = [col <= row, col >= row, col <= BLOCK - 1 - row]
    pieces = rounded(forward, 2)
    pieces += [part.astype(ml_dtypes.bfloat16) for part in sums]
    pieces += [part for pair in zip(*(rounded(half, 2) for half in inverse)) for part in pair]
    return np.concatenate(pieces, axis=0)


def rounded(values, terms):
    parts = []
    for _ in range(terms):
        part = values.astype(ml_dtypes.bfloat16)
        parts.append(part)
        values = values - part.astype(np.float64)
    return parts


def split(value, terms):
    parts = []
    for _ in range(terms - 1):
        part = value.astype(jnp.bfloat16)
        parts.append(part)
        value = value - part.astype(jnp.float32)
    return parts + [value.astype(jnp.bfloat16)]


def mm(a, b):
    return jnp.dot(a, b, preferred_element_type=jnp.float32)


def kernel(
    groups, atom_total, x, table, out,
    xv, recv, mine, sibling, total, msgs, held, drift, spectrum, acc_re, acc_im, acc_top, squares,
    load_sem, const_sem, own_sem, send_sem, recv_sem, pair_send, pair_recv, msg_send, msg_recv,
):
    me, core = lax.axis_index("frames"), lax.axis_index("atoms")
    frames = x.shape[1]
    width = recv.shape[2]
    blocks = recv.shape[1] // BLOCK
    tiles = x.shape[2] // LANES

    loads = [pltpu.make_async_copy(x.at[c], xv.at[c], load_sem.at[c]) for c in range(3)]
    for load in loads:
        load.start()
    const = pltpu.make_async_copy(table, held, const_sem)
    const.start()
    tall = 2 * BLOCK + 16

    def forward(part):
        return held[part * tall : (part + 1) * tall, :]

    def sums(which):
        start = 2 * tall + which * BLOCK
        return held[start : start + BLOCK, :]

    def inverse(part, which):
        start = 2 * tall + (3 + 2 * part + which) * BLOCK
        return held[start : start + BLOCK, :]

    def peer_at(k):
        return lax.rem(me + k, groups)

    def own_copy(c):
        return pltpu.make_async_copy(
            x.at[c, :, pl.ds(pl.multiple_of(me * width, width), width)],
            recv.at[c, pl.ds(pl.multiple_of(me * frames, frames), frames), :],
            own_sem.at[c],
        )

    barrier = pltpu.get_barrier_semaphore()

    def greet(k, carry):
        pl.semaphore_signal(barrier, inc=1, device_id={"frames": peer_at(k)}, device_id_type=MESH)
        return carry

    pl.semaphore_signal(barrier, inc=1, device_id={"atoms": 1 - core}, device_id_type=MESH)
    lax.fori_loop(1, groups, greet, 0)
    pl.semaphore_wait(barrier, groups)

    half = groups // 2
    side = me // half
    spot = lax.rem(me, half)

    def send_component(c):
        def send(t, carry):
            offset = half + (1 - 2 * lax.rem(t, 2)) * ((t + 1) // 2)
            peer = peer_at(offset)
            far = lax.rem(peer // half + side, 2)
            pltpu.make_async_remote_copy(
                src_ref=x.at[c, :, pl.ds(pl.multiple_of(peer * width, width), width)],
                dst_ref=recv.at[c, pl.ds(pl.multiple_of(me * frames, frames), frames), :],
                send_sem=send_sem.at[c, far],
                recv_sem=recv_sem.at[c, far],
                device_id={"frames": peer},
                device_id_type=MESH,
            ).start()
            return carry

        lax.fori_loop(0, groups - 1, send, 0)
        own_copy(c).start()

    send_component(0)

    parts = []
    for c in range(3):
        loads[c].wait()
        part = xv[c, :, 0:LANES]
        for tile in range(1, tiles):
            part = part + xv[c, :, tile * LANES : (tile + 1) * LANES]
        parts.append(part)
    lanes = mine.shape[1]
    if lanes > 3 * frames:
        parts.append(jnp.zeros((lanes - 3 * frames, LANES), jnp.float32))
    mine[...] = jnp.sum(jnp.transpose(jnp.concatenate(parts, axis=0)), axis=0, keepdims=True)
    pair = pltpu.make_async_remote_copy(
        src_ref=mine,
        dst_ref=sibling,
        send_sem=pair_send,
        recv_sem=pair_recv,
        device_id={"atoms": 1 - core},
        device_id_type=MESH,
    )
    pair.start()
    pair.wait()
    total[...] = (mine[...] + sibling[...]) / atom_total

    def tell(k):
        return pltpu.make_async_remote_copy(
            src_ref=total,
            dst_ref=msgs.at[me],
            send_sem=msg_send.at[k],
            recv_sem=msg_recv.at[k],
            device_id={"frames": peer_at(k)},
            device_id_type=MESH,
        )

    def tell_start(k, carry):
        tell(k).start()
        return carry

    lax.fori_loop(1, groups, tell_start, 0)
    send_component(1)
    send_component(2)
    msgs[pl.ds(me, 1)] = total[...][None]

    acc_re[...] = jnp.zeros_like(acc_re)
    acc_im[...] = jnp.zeros_like(acc_im)
    acc_top[...] = jnp.zeros_like(acc_top)
    squares[...] = jnp.zeros_like(squares)
    const.wait()

    def heard(k, carry):
        source = lax.rem(me + groups - k, groups)
        pltpu.make_async_remote_copy(
            src_ref=total,
            dst_ref=msgs.at[source],
            send_sem=msg_send.at[k],
            recv_sem=msg_recv.at[k],
            device_id={"frames": source},
            device_id_type=MESH,
        ).wait()
        return carry

    lax.fori_loop(1, groups, heard, 0)

    def spread(b, carry):
        column = jnp.transpose(jnp.broadcast_to(msgs[pl.ds(b, 1)][0], (LANES, lanes)))
        for c in range(3):
            drift[c, pl.ds(pl.multiple_of(b * frames, frames), frames), :] = column[
                c * frames : (c + 1) * frames
            ]
        return carry

    lax.fori_loop(0, groups, spread, 0)

    def several(c, far):
        return recv.at[c, pl.ds(0, (half if far else half - 1) * frames), :]

    def sent(c, far):
        gone = several(c, far)
        pltpu.make_async_copy(gone, gone, send_sem.at[c, int(far)]).wait()

    def arrived(c, far):
        came = several(c, far)
        pltpu.make_async_copy(came, came, recv_sem.at[c, int(far)]).wait()

    def lanes_of(value):
        return [value[:, i : i + width] for i in range(0, value.shape[1], width)]

    def transform(c, which):
        pieces = []
        for i in range(blocks // 2):
            at = pl.ds(pl.multiple_of((which * (blocks // 2) + i) * BLOCK, BLOCK), BLOCK)
            pieces.append(recv[c, at, :] - drift[c, at, :])
        high, low = split(jnp.concatenate(pieces, axis=1), 2)
        running = mm(sums(0), high) + mm(sums(0), low)
        first, second = lanes_of(running[BLOCK - 1 : BLOCK, :])
        later = jnp.full((1, 1), which, jnp.int32).astype(jnp.float32)
        sooner = 1.0 - later
        shift = jnp.concatenate([-sooner * (first + second), later * first - sooner * second], axis=1)
        positions = running + shift
        squares[which] += positions * positions
        high, low = split(positions, 2)
        spectrum[which] = mm(forward(0), high) + (mm(forward(0), low) + mm(forward(1), high))

    def spectra(at):
        return lanes_of(spectrum[0, at, :]) + lanes_of(spectrum[1, at, :])

    def component(c, carry):
        own_copy(c).wait()
        arrived(c, False)
        transform(c, side)
        arrived(c, True)
        transform(c, 1 - side)

        def rows(r, inner):
            at = pl.ds(pl.multiple_of(r * 8, 8), 8)
            re = spectra(at)
            im = spectra(pl.ds(pl.multiple_of(BLOCK + r * 8, 8), 8))
            for d in range(blocks):
                here = slice(d * width, (d + 1) * width)
                real = acc_re[at, here]
                imag = acc_im[at, here]
                for i in range(blocks - d):
                    j = i + d
                    real = real + (re[i] * re[j] + im[i] * im[j])
                    if d:
                        imag = imag + (re[i] * im[j] - im[i] * re[j])
                acc_re[at, here] = real
                if d:
                    acc_im[at, here] = imag
            return inner

        lax.fori_loop(0, BLOCK // 8, rows, 0, unroll=4)
        top = spectra(pl.ds(2 * BLOCK, 8))
        for d in range(blocks):
            here = slice(d * width, (d + 1) * width)
            value = acc_top[:, here]
            for i in range(blocks - d):
                value = value + top[i] * top[i + d]
            acc_top[:, here] = value
        return carry

    lax.fori_loop(0, 3, component, 0)

    def next_block(value):
        return jnp.concatenate([value[:, width:], jnp.zeros_like(value[:, :width])], axis=1)

    parity = (1 - 2 * (lax.broadcasted_iota(jnp.int32, (BLOCK, 1), 0) % 2)).astype(jnp.float32)
    real, imag, top = acc_re[...], acc_im[...], acc_top[0:1, :]
    cross = [split(real + parity * next_block(real), 2), split(imag + parity * next_block(imag), 2)]
    corr = jnp.zeros_like(real)
    for a, b in ((1, 0), (0, 1), (0, 0)):
        corr = corr + (mm(inverse(a, 0), cross[0][b]) + mm(inverse(a, 1), cross[1][b]))
    corr = corr - (top + next_block(top)) * (parity * (1.0 / BLOCK))
    parts = split(jnp.concatenate([squares[0], squares[1]], axis=1), 2)
    later = mm(sums(1), parts[0]) + mm(sums(1), parts[1])
    parts = [jnp.concatenate(lanes_of(part)[::-1], axis=1) for part in parts]
    earlier = mm(sums(2), parts[0]) + mm(sums(2), parts[1])
    sums_of = lanes_of(later[0:1, :])
    whole = []
    for i in range(blocks):
        value = jnp.zeros((1, width), jnp.float32)
        for j in list(range(i + 1, blocks)) + list(range(blocks - 1 - i)):
            value = value + sums_of[j]
        whole.append(value)
    result = later + earlier + jnp.concatenate(whole, axis=1) + corr
    for i, piece in enumerate(lanes_of(result)):
        lag = i * BLOCK + lax.broadcasted_iota(jnp.int32, (BLOCK, 1), 0)
        pairs = (blocks * BLOCK - lag).astype(jnp.float32)
        out[:, i * BLOCK : (i + 1) * BLOCK] = jnp.transpose(piece / pairs)

    for c in range(3):
        sent(c, False)
        sent(c, True)


def fused(displacements):
    frames, _, atom_count = displacements.shape
    groups = lax.axis_size("frames")
    length = frames * groups
    width = atom_count // groups
    blocks = length // BLOCK
    table = tables()
    lanes = -(-3 * frames // LANES) * LANES
    f32, bf16 = jnp.float32, jnp.bfloat16
    dma = pltpu.SemaphoreType.DMA
    result = pl.pallas_call(
        functools.partial(kernel, groups, atom_count * lax.axis_size("atoms")),
        out_shape=jax.ShapeDtypeStruct((width, length), f32),
        in_specs=[pl.BlockSpec(memory_space=pltpu.HBM)] * 2,
        out_specs=pl.BlockSpec(memory_space=pltpu.VMEM),
        scratch_shapes=[
            pltpu.VMEM((3, frames, atom_count), f32),
            pltpu.VMEM((3, length, width), f32),
            pltpu.VMEM((1, lanes), f32),
            pltpu.VMEM((1, lanes), f32),
            pltpu.VMEM((1, lanes), f32),
            pltpu.VMEM((groups, 1, lanes), f32),
            pltpu.VMEM(table.shape, bf16),
            pltpu.VMEM((3, length, width), f32),
            pltpu.VMEM((2, 2 * BLOCK + 16, blocks * width // 2), f32),
            pltpu.VMEM((BLOCK, blocks * width), f32),
            pltpu.VMEM((BLOCK, blocks * width), f32),
            pltpu.VMEM((8, blocks * width), f32),
            pltpu.VMEM((2, BLOCK, blocks * width // 2), f32),
            dma((3,)), dma, dma((3,)), dma((3, 2)), dma((3, 2)),
            dma, dma, dma((groups,)), dma((groups,)),
        ],
        compiler_params=pltpu.CompilerParams(
            collective_id=0, has_side_effects=True, vmem_limit_bytes=60 * 1024 * 1024
        ),
    )(jnp.transpose(displacements, (1, 0, 2)), jnp.asarray(table))
    return pl.pallas_call(
        deliver,
        out_shape=jax.ShapeDtypeStruct((width, length), f32),
        in_specs=[pl.BlockSpec(memory_space=pltpu.HBM)],
        out_specs=pl.BlockSpec(memory_space=pltpu.HBM),
        scratch_shapes=[dma((PIECES,))],
    )(result)


def deliver(source, target, sem):
    rows = source.shape[0] // PIECES
    copies = [
        pltpu.make_async_copy(
            source.at[pl.ds(i * rows, rows), :], target.at[pl.ds(i * rows, rows), :], sem.at[i]
        )
        for i in range(PIECES)
    ]
    for copy in copies:
        copy.start()
    for copy in copies:
        copy.wait()


def fits(mesh, shape):
    groups, pairs = mesh.shape["frames"], mesh.shape["atoms"]
    length, _, atoms = shape
    if pairs != 2 or groups % 2 or atoms != pairs * groups * LANES or length != 4 * BLOCK:
        return False
    return length // groups % 8 == 0


def solution(mesh):
    def run(displacements):
        return jax.shard_map(
            fused if fits(mesh, displacements.shape) else per_device,
            mesh=mesh,
            in_specs=(P("frames", None, "atoms"),),
            out_specs=P(("atoms", "frames"), None),
            check_vma=False,
        )(displacements)

    return run
```

```python
import functools
import math

import jax
import jax.numpy as jnp
import ml_dtypes
import numpy as np
from jax import lax
from jax.experimental import pallas as pl
from jax.experimental.pallas import tpu as pltpu
from jax.sharding import PartitionSpec as P


BLOCK = 256
LANES = 128
PIECES = 4
MESH = pl.DeviceIdType.MESH


def carried_in(array, axis, combine, identity):
    count, index = (lax.axis_size(axis), lax.axis_index(axis))
    everything = lax.all_gather(array, axis)
    start = jnp.broadcast_to(jnp.asarray(identity, array.dtype), array.shape)

    def hop(k, before):
        reached = k < index
        new = combine(before, everything[k])
        return jnp.where(reached, new, before)

    return lax.fori_loop(0, count, hop, start)


def lag_table(positions):
    length = positions.shape[0]
    count = positions.shape[3]
    series = positions.reshape(length, 3 * count)
    squares = jnp.sum(positions * positions, axis=(1, 2))
    zero_row = jnp.zeros((1, count), jnp.float32)
    running = jnp.concatenate([zero_row, jnp.cumsum(squares, axis=0)], axis=0)
    head = running[length][None, :] - running[:length]
    tail = jnp.flip(running[1:], 0)
    block = min(256, length)
    frame = jnp.arange(length, dtype=jnp.int32)
    starts = jnp.arange(0, length, block, dtype=jnp.int32)

    def add_block(corr, start):
        freq = start + jnp.arange(block, dtype=jnp.int32)
        phase = frame[:, None] * freq[None, :] % (2 * length)
        angle = phase.astype(jnp.float32) * (math.pi / length)
        cosine = jnp.cos(angle)
        sine = jnp.sin(angle)
        real_part = lax.dot_general(
            series, cosine, (((0,), (0,)), ((), ())), precision=lax.Precision.HIGHEST
        )
        imag_part = lax.dot_general(
            series, sine, (((0,), (0,)), ((), ())), precision=lax.Precision.HIGHEST
        )
        power = jnp.sum(
            (real_part * real_part + imag_part * imag_part).reshape(3, count, block), axis=0
        )
        weight = jnp.where(freq == 0, 1.0, 2.0).astype(jnp.float32) / (2.0 * length)
        term = lax.dot_general(
            power * weight[None, :],
            cosine,
            (((1,), (1,)), ((), ())),
            precision=lax.Precision.HIGHEST,
        )
        return (corr + term, None)

    corr, _ = lax.scan(add_block, jnp.zeros((count, length), jnp.float32), starts)
    parity = jnp.where(frame % 2 == 0, 1.0, -1.0).astype(jnp.float32)
    highest = jnp.dot(parity, series, precision=lax.Precision.HIGHEST)
    power_top = jnp.sum((highest * highest).reshape(3, count), axis=0)
    corr = corr + power_top[:, None] * parity[None, :] / (2.0 * length)
    counts = (length - frame).astype(jnp.float32)
    return (jnp.transpose(head + tail) - 2.0 * corr) / counts[None, :]


def add_carry(earlier, later):
    return earlier + later


def per_device(displacements):
    local_frames, _, atom_count = displacements.shape
    groups = lax.axis_size("frames")
    atom_total = atom_count * lax.axis_size("atoms")
    summed = lax.psum(jnp.sum(displacements, axis=2), "atoms")
    centred = displacements - (summed / atom_total)[:, :, None]
    partial_value = jnp.cumsum(centred, axis=0)
    earlier = carried_in(partial_value[-1], "frames", add_carry, jnp.zeros_like(partial_value[-1]))
    positions = (partial_value + earlier[None]).reshape(
        local_frames, 3, groups, atom_count // groups
    )
    return lag_table(lax.all_to_all(positions, "frames", split_axis=2, concat_axis=0, tiled=True))


def tables():
    points = 2 * BLOCK
    index = np.arange(BLOCK)
    angle = 2.0 * np.pi * (np.outer(index, index) % points) / points
    forward = np.zeros((points + 16, BLOCK))
    forward[:BLOCK] = np.cos(angle)
    forward[BLOCK:points] = -np.sin(angle)
    forward[points] = 1.0 - 2.0 * (index % 2)
    weight = np.where(index == 0, 1.0, 2.0)[None, :] / points
    inverse = [-2.0 * np.cos(angle) * weight, 2.0 * np.sin(angle) * weight]
    row, col = index[:, None], index[None, :]
    sums = [col <= row, col >= row, col <= BLOCK - 1 - row]
    pieces = rounded(forward, 2)
    pieces += [part.astype(ml_dtypes.bfloat16) for part in sums]
    pieces += [part for pair in zip(*(rounded(half, 2) for half in inverse)) for part in pair]
    return np.concatenate(pieces, axis=0)


def rounded(values, terms):
    parts = []
    for _ in range(terms):
        part = values.astype(ml_dtypes.bfloat16)
        parts.append(part)
        values = values - part.astype(np.float64)
    return parts


def split(value, terms):
    parts = []
    for _ in range(terms - 1):
        part = value.astype(jnp.bfloat16)
        parts.append(part)
        value = value - part.astype(jnp.float32)
    return parts + [value.astype(jnp.bfloat16)]


def mm(a, b):
    return jnp.dot(a, b, preferred_element_type=jnp.float32)


def kernel(
    groups, atom_total, x, table, out,
    xv, recv, mine, sibling, total, msgs, held, drift, spectrum, acc_re, acc_im, acc_top, squares,
    load_sem, const_sem, own_sem, send_sem, recv_sem, pair_send, pair_recv, msg_send, msg_recv,
):
    me, core = lax.axis_index("frames"), lax.axis_index("atoms")
    frames = x.shape[1]
    width = recv.shape[2]
    blocks = recv.shape[1] // BLOCK
    tiles = x.shape[2] // LANES

    loads = [pltpu.make_async_copy(x.at[c], xv.at[c], load_sem.at[c]) for c in range(3)]
    for load in loads:
        load.start()
    const = pltpu.make_async_copy(table, held, const_sem)
    const.start()
    tall = 2 * BLOCK + 16

    def forward(part):
        return held[part * tall : (part + 1) * tall, :]

    def sums(which):
        start = 2 * tall + which * BLOCK
        return held[start : start + BLOCK, :]

    def inverse(part, which):
        start = 2 * tall + (3 + 2 * part + which) * BLOCK
        return held[start : start + BLOCK, :]

    def peer_at(k):
        return lax.rem(me + k, groups)

    def own_copy(c):
        return pltpu.make_async_copy(
            x.at[c, :, pl.ds(pl.multiple_of(me * width, width), width)],
            recv.at[c, pl.ds(pl.multiple_of(me * frames, frames), frames), :],
            own_sem.at[c],
        )

    barrier = pltpu.get_barrier_semaphore()

    def greet(k, carry):
        pl.semaphore_signal(barrier, inc=1, device_id={"frames": peer_at(k)}, device_id_type=MESH)
        return carry

    pl.semaphore_signal(barrier, inc=1, device_id={"atoms": 1 - core}, device_id_type=MESH)
    lax.fori_loop(1, groups, greet, 0)
    pl.semaphore_wait(barrier, groups)

    half = groups // 2
    side = me // half
    spot = lax.rem(me, half)

    def send_component(c):
        def send(t, carry):
            offset = half + (1 - 2 * lax.rem(t, 2)) * ((t + 1) // 2)
            peer = peer_at(offset)
            far = lax.rem(peer // half + side, 2)
            pltpu.make_async_remote_copy(
                src_ref=x.at[c, :, pl.ds(pl.multiple_of(peer * width, width), width)],
                dst_ref=recv.at[c, pl.ds(pl.multiple_of(me * frames, frames), frames), :],
                send_sem=send_sem.at[c, far],
                recv_sem=recv_sem.at[c, far],
                device_id={"frames": peer},
                device_id_type=MESH,
            ).start()
            return carry

        lax.fori_loop(0, groups - 1, send, 0)
        own_copy(c).start()

    send_component(0)

    parts = []
    for c in range(3):
        loads[c].wait()
        part = xv[c, :, 0:LANES]
        for tile in range(1, tiles):
            part = part + xv[c, :, tile * LANES : (tile + 1) * LANES]
        parts.append(part)
    lanes = mine.shape[1]
    if lanes > 3 * frames:
        parts.append(jnp.zeros((lanes - 3 * frames, LANES), jnp.float32))
    mine[...] = jnp.sum(jnp.transpose(jnp.concatenate(parts, axis=0)), axis=0, keepdims=True)
    pair = pltpu.make_async_remote_copy(
        src_ref=mine,
        dst_ref=sibling,
        send_sem=pair_send,
        recv_sem=pair_recv,
        device_id={"atoms": 1 - core},
        device_id_type=MESH,
    )
    pair.start()
    pair.wait()
    total[...] = (mine[...] + sibling[...]) / atom_total

    def tell(k):
        return pltpu.make_async_remote_copy(
            src_ref=total,
            dst_ref=msgs.at[me],
            send_sem=msg_send.at[k],
            recv_sem=msg_recv.at[k],
            device_id={"frames": peer_at(k)},
            device_id_type=MESH,
        )

    def tell_start(k, carry):
        tell(k).start()
        return carry

    lax.fori_loop(1, groups, tell_start, 0)
    send_component(1)
    send_component(2)
    msgs[pl.ds(me, 1)] = total[...][None]

    acc_re[...] = jnp.zeros_like(acc_re)
    acc_im[...] = jnp.zeros_like(acc_im)
    acc_top[...] = jnp.zeros_like(acc_top)
    squares[...] = jnp.zeros_like(squares)
    const.wait()

    def heard(k, carry):
        source = lax.rem(me + groups - k, groups)
        pltpu.make_async_remote_copy(
            src_ref=total,
            dst_ref=msgs.at[source],
            send_sem=msg_send.at[k],
            recv_sem=msg_recv.at[k],
            device_id={"frames": source},
            device_id_type=MESH,
        ).wait()
        return carry

    lax.fori_loop(1, groups, heard, 0)

    def spread(b, carry):
        column = jnp.transpose(jnp.broadcast_to(msgs[pl.ds(b, 1)][0], (LANES, lanes)))
        for c in range(3):
            drift[c, pl.ds(pl.multiple_of(b * frames, frames), frames), :] = column[
                c * frames : (c + 1) * frames
            ]
        return carry

    lax.fori_loop(0, groups, spread, 0)

    def several(c, far):
        return recv.at[c, pl.ds(0, (half if far else half - 1) * frames), :]

    def sent(c, far):
        gone = several(c, far)
        pltpu.make_async_copy(gone, gone, send_sem.at[c, int(far)]).wait()

    def arrived(c, far):
        came = several(c, far)
        pltpu.make_async_copy(came, came, recv_sem.at[c, int(far)]).wait()

    def lanes_of(value):
        return [value[:, i : i + width] for i in range(0, value.shape[1], width)]

    def transform(c, which):
        pieces = []
        for i in range(blocks // 2):
            at = pl.ds(pl.multiple_of((which * (blocks // 2) + i) * BLOCK, BLOCK), BLOCK)
            pieces.append(recv[c, at, :] - drift[c, at, :])
        high, low = split(jnp.concatenate(pieces, axis=1), 2)
        running = mm(sums(0), high) + mm(sums(0), low)
        first, second = lanes_of(running[BLOCK - 1 : BLOCK, :])
        later = jnp.full((1, 1), which, jnp.int32).astype(jnp.float32)
        sooner = 1.0 - later
        shift = jnp.concatenate([-sooner * (first + second), later * first - sooner * second], axis=1)
        positions = running + shift
        squares[which] += positions * positions
        high, low = split(positions, 2)
        spectrum[which] = mm(forward(0), high) + (mm(forward(0), low) + mm(forward(1), high))

    def spectra(at):
        return lanes_of(spectrum[0, at, :]) + lanes_of(spectrum[1, at, :])

    def component(c, carry):
        own_copy(c).wait()
        arrived(c, False)
        transform(c, side)
        arrived(c, True)
        transform(c, 1 - side)

        def rows(r, inner):
            at = pl.ds(pl.multiple_of(r * 8, 8), 8)
            re = spectra(at)
            im = spectra(pl.ds(pl.multiple_of(BLOCK + r * 8, 8), 8))
            for d in range(blocks):
                here = slice(d * width, (d + 1) * width)
                real = acc_re[at, here]
                imag = acc_im[at, here]
                for i in range(blocks - d):
                    j = i + d
                    real = real + (re[i] * re[j] + im[i] * im[j])
                    if d:
                        imag = imag + (re[i] * im[j] - im[i] * re[j])
                acc_re[at, here] = real
                if d:
                    acc_im[at, here] = imag
            return inner

        lax.fori_loop(0, BLOCK // 8, rows, 0, unroll=4)
        top = spectra(pl.ds(2 * BLOCK, 8))
        for d in range(blocks):
            here = slice(d * width, (d + 1) * width)
            value = acc_top[:, here]
            for i in range(blocks - d):
                value = value + top[i] * top[i + d]
            acc_top[:, here] = value
        return carry

    lax.fori_loop(0, 3, component, 0)

    def next_block(value):
        return jnp.concatenate([value[:, width:], jnp.zeros_like(value[:, :width])], axis=1)

    parity = (1 - 2 * (lax.broadcasted_iota(jnp.int32, (BLOCK, 1), 0) % 2)).astype(jnp.float32)
    real, imag, top = acc_re[...], acc_im[...], acc_top[0:1, :]
    cross = [split(real + parity * next_block(real), 2), split(imag + parity * next_block(imag), 2)]
    corr = jnp.zeros_like(real)
    for a, b in ((1, 0), (0, 1), (0, 0)):
        corr = corr + (mm(inverse(a, 0), cross[0][b]) + mm(inverse(a, 1), cross[1][b]))
    corr = corr - (top + next_block(top)) * (parity * (1.0 / BLOCK))
    parts = split(jnp.concatenate([squares[0], squares[1]], axis=1), 2)
    later = mm(sums(1), parts[0]) + mm(sums(1), parts[1])
    parts = [jnp.concatenate(lanes_of(part)[::-1], axis=1) for part in parts]
    earlier = mm(sums(2), parts[0]) + mm(sums(2), parts[1])
    sums_of = lanes_of(later[0:1, :])
    whole = []
    for i in range(blocks):
        value = jnp.zeros((1, width), jnp.float32)
        for j in list(range(i + 1, blocks)) + list(range(blocks - 1 - i)):
            value = value + sums_of[j]
        whole.append(value)
    result = later + earlier + jnp.concatenate(whole, axis=1) + corr
    for i, piece in enumerate(lanes_of(result)):
        lag = i * BLOCK + lax.broadcasted_iota(jnp.int32, (BLOCK, 1), 0)
        pairs = (blocks * BLOCK - lag).astype(jnp.float32)
        out[:, i * BLOCK : (i + 1) * BLOCK] = jnp.transpose(piece / pairs)

    for c in range(3):
        sent(c, False)
        sent(c, True)


def fused(displacements):
    frames, _, atom_count = displacements.shape
    groups = lax.axis_size("frames")
    length = frames * groups
    width = atom_count // groups
    blocks = length // BLOCK
    table = tables()
    lanes = -(-3 * frames // LANES) * LANES
    f32, bf16 = jnp.float32, jnp.bfloat16
    dma = pltpu.SemaphoreType.DMA
    result = pl.pallas_call(
        functools.partial(kernel, groups, atom_count * lax.axis_size("atoms")),
        out_shape=jax.ShapeDtypeStruct((width, length), f32),
        in_specs=[pl.BlockSpec(memory_space=pltpu.HBM)] * 2,
        out_specs=pl.BlockSpec(memory_space=pltpu.VMEM),
        scratch_shapes=[
            pltpu.VMEM((3, frames, atom_count), f32),
            pltpu.VMEM((3, length, width), f32),
            pltpu.VMEM((1, lanes), f32),
            pltpu.VMEM((1, lanes), f32),
            pltpu.VMEM((1, lanes), f32),
            pltpu.VMEM((groups, 1, lanes), f32),
            pltpu.VMEM(table.shape, bf16),
            pltpu.VMEM((3, length, width), f32),
            pltpu.VMEM((2, 2 * BLOCK + 16, blocks * width // 2), f32),
            pltpu.VMEM((BLOCK, blocks * width), f32),
            pltpu.VMEM((BLOCK, blocks * width), f32),
            pltpu.VMEM((8, blocks * width), f32),
            pltpu.VMEM((2, BLOCK, blocks * width // 2), f32),
            dma((3,)), dma, dma((3,)), dma((3, 2)), dma((3, 2)),
            dma, dma, dma((groups,)), dma((groups,)),
        ],
        compiler_params=pltpu.CompilerParams(
            collective_id=0, has_side_effects=True, vmem_limit_bytes=60 * 1024 * 1024
        ),
    )(jnp.transpose(displacements, (1, 0, 2)), jnp.asarray(table))
    return pl.pallas_call(
        deliver,
        out_shape=jax.ShapeDtypeStruct((width, length), f32),
        in_specs=[pl.BlockSpec(memory_space=pltpu.HBM)],
        out_specs=pl.BlockSpec(memory_space=pltpu.HBM),
        scratch_shapes=[pltpu.VMEM((width, length), f32), dma((PIECES,)), dma((PIECES,))],
    )(result)


def deliver(source, target, held, come, go):
    rows = source.shape[0] // PIECES
    here = [pl.ds(i * rows, rows) for i in range(PIECES)]
    inward = [
        pltpu.make_async_copy(source.at[at, :], held.at[at, :], come.at[i]) for i, at in enumerate(here)
    ]
    outward = [
        pltpu.make_async_copy(held.at[at, :], target.at[at, :], go.at[i]) for i, at in enumerate(here)
    ]
    for copy in inward:
        copy.start()
    for before, after in zip(inward, outward):
        before.wait()
        after.start()
    for copy in outward:
        copy.wait()


def fits(mesh, shape):
    groups, pairs = mesh.shape["frames"], mesh.shape["atoms"]
    length, _, atoms = shape
    if pairs != 2 or groups % 2 or atoms != pairs * groups * LANES or length != 4 * BLOCK:
        return False
    return length // groups % 8 == 0


def solution(mesh):
    def run(displacements):
        return jax.shard_map(
            fused if fits(mesh, displacements.shape) else per_device,
            mesh=mesh,
            in_specs=(P("frames", None, "atoms"),),
            out_specs=P(("atoms", "frames"), None),
            check_vma=False,
        )(displacements)

    return run
```

```python
import functools
import math

import jax
import jax.numpy as jnp
import ml_dtypes
import numpy as np
from jax import lax
from jax.experimental import pallas as pl
from jax.experimental.pallas import tpu as pltpu
from jax.sharding import PartitionSpec as P


BLOCK = 256
LANES = 128
MESH = pl.DeviceIdType.MESH


def carried_in(array, axis, combine, identity):
    count, index = (lax.axis_size(axis), lax.axis_index(axis))
    everything = lax.all_gather(array, axis)
    start = jnp.broadcast_to(jnp.asarray(identity, array.dtype), array.shape)

    def hop(k, before):
        reached = k < index
        new = combine(before, everything[k])
        return jnp.where(reached, new, before)

    return lax.fori_loop(0, count, hop, start)


def lag_table(positions):
    length = positions.shape[0]
    count = positions.shape[3]
    series = positions.reshape(length, 3 * count)
    squares = jnp.sum(positions * positions, axis=(1, 2))
    zero_row = jnp.zeros((1, count), jnp.float32)
    running = jnp.concatenate([zero_row, jnp.cumsum(squares, axis=0)], axis=0)
    head = running[length][None, :] - running[:length]
    tail = jnp.flip(running[1:], 0)
    block = min(256, length)
    frame = jnp.arange(length, dtype=jnp.int32)
    starts = jnp.arange(0, length, block, dtype=jnp.int32)

    def add_block(corr, start):
        freq = start + jnp.arange(block, dtype=jnp.int32)
        phase = frame[:, None] * freq[None, :] % (2 * length)
        angle = phase.astype(jnp.float32) * (math.pi / length)
        cosine = jnp.cos(angle)
        sine = jnp.sin(angle)
        real_part = lax.dot_general(
            series, cosine, (((0,), (0,)), ((), ())), precision=lax.Precision.HIGHEST
        )
        imag_part = lax.dot_general(
            series, sine, (((0,), (0,)), ((), ())), precision=lax.Precision.HIGHEST
        )
        power = jnp.sum(
            (real_part * real_part + imag_part * imag_part).reshape(3, count, block), axis=0
        )
        weight = jnp.where(freq == 0, 1.0, 2.0).astype(jnp.float32) / (2.0 * length)
        term = lax.dot_general(
            power * weight[None, :],
            cosine,
            (((1,), (1,)), ((), ())),
            precision=lax.Precision.HIGHEST,
        )
        return (corr + term, None)

    corr, _ = lax.scan(add_block, jnp.zeros((count, length), jnp.float32), starts)
    parity = jnp.where(frame % 2 == 0, 1.0, -1.0).astype(jnp.float32)
    highest = jnp.dot(parity, series, precision=lax.Precision.HIGHEST)
    power_top = jnp.sum((highest * highest).reshape(3, count), axis=0)
    corr = corr + power_top[:, None] * parity[None, :] / (2.0 * length)
    counts = (length - frame).astype(jnp.float32)
    return (jnp.transpose(head + tail) - 2.0 * corr) / counts[None, :]


def add_carry(earlier, later):
    return earlier + later


def per_device(displacements):
    local_frames, _, atom_count = displacements.shape
    groups = lax.axis_size("frames")
    atom_total = atom_count * lax.axis_size("atoms")
    summed = lax.psum(jnp.sum(displacements, axis=2), "atoms")
    centred = displacements - (summed / atom_total)[:, :, None]
    partial_value = jnp.cumsum(centred, axis=0)
    earlier = carried_in(partial_value[-1], "frames", add_carry, jnp.zeros_like(partial_value[-1]))
    positions = (partial_value + earlier[None]).reshape(
        local_frames, 3, groups, atom_count // groups
    )
    return lag_table(lax.all_to_all(positions, "frames", split_axis=2, concat_axis=0, tiled=True))


def tables():
    points = 2 * BLOCK
    index = np.arange(BLOCK)
    angle = 2.0 * np.pi * (np.outer(index, index) % points) / points
    forward = np.zeros((points + 16, BLOCK))
    forward[:BLOCK] = np.cos(angle)
    forward[BLOCK:points] = -np.sin(angle)
    forward[points] = 1.0 - 2.0 * (index % 2)
    weight = np.where(index == 0, 1.0, 2.0)[None, :] / points
    inverse = [-2.0 * np.cos(angle) * weight, 2.0 * np.sin(angle) * weight]
    row, col = index[:, None], index[None, :]
    sums = [col <= row, col >= row, col <= BLOCK - 1 - row]
    pieces = rounded(forward, 2)
    pieces += [part.astype(ml_dtypes.bfloat16) for part in sums]
    pieces += [part for pair in zip(*(rounded(half, 3) for half in inverse)) for part in pair]
    return np.concatenate(pieces, axis=0)


def rounded(values, terms):
    parts = []
    for _ in range(terms):
        part = values.astype(ml_dtypes.bfloat16)
        parts.append(part)
        values = values - part.astype(np.float64)
    return parts


def split(value, terms):
    parts = []
    for _ in range(terms - 1):
        part = value.astype(jnp.bfloat16)
        parts.append(part)
        value = value - part.astype(jnp.float32)
    return parts + [value.astype(jnp.bfloat16)]


def mm(a, b):
    return jnp.dot(a, b, preferred_element_type=jnp.float32)


def kernel(
    groups, atom_total, x, table, out,
    xv, recv, mine, sibling, total, msgs, held, drift, spectrum, acc_re, acc_im, acc_top, squares,
    load_sem, const_sem, own_sem, send_sem, recv_sem, pair_send, pair_recv, msg_send, msg_recv,
):
    me, core = lax.axis_index("frames"), lax.axis_index("atoms")
    frames = x.shape[1]
    width = recv.shape[2]
    blocks = recv.shape[1] // BLOCK
    tiles = x.shape[2] // LANES

    loads = [pltpu.make_async_copy(x.at[c], xv.at[c], load_sem.at[c]) for c in range(3)]
    for load in loads:
        load.start()
    const = pltpu.make_async_copy(table, held, const_sem)
    const.start()
    tall = 2 * BLOCK + 16

    def forward(part):
        return held[part * tall : (part + 1) * tall, :]

    def sums(which):
        start = 2 * tall + which * BLOCK
        return held[start : start + BLOCK, :]

    def inverse(part, which):
        start = 2 * tall + (3 + 2 * part + which) * BLOCK
        return held[start : start + BLOCK, :]

    def peer_at(k):
        return lax.rem(me + k, groups)

    def own_copy(c):
        return pltpu.make_async_copy(
            x.at[c, :, pl.ds(pl.multiple_of(me * width, width), width)],
            recv.at[c, pl.ds(pl.multiple_of(me * frames, frames), frames), :],
            own_sem.at[c],
        )

    barrier = pltpu.get_barrier_semaphore()

    def greet(k, carry):
        pl.semaphore_signal(barrier, inc=1, device_id={"frames": peer_at(k)}, device_id_type=MESH)
        return carry

    pl.semaphore_signal(barrier, inc=1, device_id={"atoms": 1 - core}, device_id_type=MESH)
    lax.fori_loop(1, groups, greet, 0)
    pl.semaphore_wait(barrier, groups)

    half = groups // 2
    side = me // half
    spot = lax.rem(me, half)

    def send_component(c):
        def send(t, carry):
            offset = half + (1 - 2 * lax.rem(t, 2)) * ((t + 1) // 2)
            peer = peer_at(offset)
            far = lax.rem(peer // half + side, 2)
            pltpu.make_async_remote_copy(
                src_ref=x.at[c, :, pl.ds(pl.multiple_of(peer * width, width), width)],
                dst_ref=recv.at[c, pl.ds(pl.multiple_of(me * frames, frames), frames), :],
                send_sem=send_sem.at[c, far],
                recv_sem=recv_sem.at[c, far],
                device_id={"frames": peer},
                device_id_type=MESH,
            ).start()
            return carry

        lax.fori_loop(0, groups - 1, send, 0)
        own_copy(c).start()

    send_component(0)

    parts = []
    for c in range(3):
        loads[c].wait()
        part = xv[c, :, 0:LANES]
        for tile in range(1, tiles):
            part = part + xv[c, :, tile * LANES : (tile + 1) * LANES]
        parts.append(part)
    lanes = mine.shape[1]
    if lanes > 3 * frames:
        parts.append(jnp.zeros((lanes - 3 * frames, LANES), jnp.float32))
    mine[...] = jnp.sum(jnp.transpose(jnp.concatenate(parts, axis=0)), axis=0, keepdims=True)
    pair = pltpu.make_async_remote_copy(
        src_ref=mine,
        dst_ref=sibling,
        send_sem=pair_send,
        recv_sem=pair_recv,
        device_id={"atoms": 1 - core},
        device_id_type=MESH,
    )
    pair.start()
    pair.wait()
    total[...] = (mine[...] + sibling[...]) / atom_total

    def tell(k):
        return pltpu.make_async_remote_copy(
            src_ref=total,
            dst_ref=msgs.at[me],
            send_sem=msg_send.at[k],
            recv_sem=msg_recv.at[k],
            device_id={"frames": peer_at(k)},
            device_id_type=MESH,
        )

    def tell_start(k, carry):
        tell(k).start()
        return carry

    lax.fori_loop(1, groups, tell_start, 0)
    send_component(1)
    send_component(2)
    msgs[pl.ds(me, 1)] = total[...][None]

    acc_re[...] = jnp.zeros_like(acc_re)
    acc_im[...] = jnp.zeros_like(acc_im)
    acc_top[...] = jnp.zeros_like(acc_top)
    squares[...] = jnp.zeros_like(squares)
    const.wait()

    def heard(k, carry):
        source = lax.rem(me + groups - k, groups)
        pltpu.make_async_remote_copy(
            src_ref=total,
            dst_ref=msgs.at[source],
            send_sem=msg_send.at[k],
            recv_sem=msg_recv.at[k],
            device_id={"frames": source},
            device_id_type=MESH,
        ).wait()
        return carry

    lax.fori_loop(1, groups, heard, 0)

    def spread(b, carry):
        column = jnp.transpose(jnp.broadcast_to(msgs[pl.ds(b, 1)][0], (LANES, lanes)))
        for c in range(3):
            drift[c, pl.ds(pl.multiple_of(b * frames, frames), frames), :] = column[
                c * frames : (c + 1) * frames
            ]
        return carry

    lax.fori_loop(0, groups, spread, 0)

    def several(c, far):
        return recv.at[c, pl.ds(0, (half if far else half - 1) * frames), :]

    def sent(c, far):
        gone = several(c, far)
        pltpu.make_async_copy(gone, gone, send_sem.at[c, int(far)]).wait()

    def arrived(c, far):
        came = several(c, far)
        pltpu.make_async_copy(came, came, recv_sem.at[c, int(far)]).wait()

    def lanes_of(value):
        return [value[:, i : i + width] for i in range(0, value.shape[1], width)]

    def transform(c, which):
        pieces = []
        for i in range(blocks // 2):
            at = pl.ds(pl.multiple_of((which * (blocks // 2) + i) * BLOCK, BLOCK), BLOCK)
            pieces.append(recv[c, at, :] - drift[c, at, :])
        high, low = split(jnp.concatenate(pieces, axis=1), 2)
        running = mm(sums(0), high) + mm(sums(0), low)
        first, second = lanes_of(running[BLOCK - 1 : BLOCK, :])
        later = jnp.full((1, 1), which, jnp.int32).astype(jnp.float32)
        sooner = 1.0 - later
        shift = jnp.concatenate([-sooner * (first + second), later * first - sooner * second], axis=1)
        positions = running + shift
        squares[which] += positions * positions
        high, low = split(positions, 2)
        spectrum[which] = mm(forward(0), high) + (mm(forward(0), low) + mm(forward(1), high))

    def spectra(at):
        return lanes_of(spectrum[0, at, :]) + lanes_of(spectrum[1, at, :])

    def component(c, carry):
        own_copy(c).wait()
        arrived(c, False)
        transform(c, side)
        arrived(c, True)
        transform(c, 1 - side)

        def rows(r, inner):
            at = pl.ds(pl.multiple_of(r * 8, 8), 8)
            re = spectra(at)
            im = spectra(pl.ds(pl.multiple_of(BLOCK + r * 8, 8), 8))
            for d in range(blocks):
                here = slice(d * width, (d + 1) * width)
                real = acc_re[at, here]
                imag = acc_im[at, here]
                for i in range(blocks - d):
                    j = i + d
                    real = real + (re[i] * re[j] + im[i] * im[j])
                    if d:
                        imag = imag + (re[i] * im[j] - im[i] * re[j])
                acc_re[at, here] = real
                if d:
                    acc_im[at, here] = imag
            return inner

        lax.fori_loop(0, BLOCK // 8, rows, 0, unroll=4)
        top = spectra(pl.ds(2 * BLOCK, 8))
        for d in range(blocks):
            here = slice(d * width, (d + 1) * width)
            value = acc_top[:, here]
            for i in range(blocks - d):
                value = value + top[i] * top[i + d]
            acc_top[:, here] = value
        return carry

    lax.fori_loop(0, 3, component, 0)

    def next_block(value):
        return jnp.concatenate([value[:, width:], jnp.zeros_like(value[:, :width])], axis=1)

    parity = (1 - 2 * (lax.broadcasted_iota(jnp.int32, (BLOCK, 1), 0) % 2)).astype(jnp.float32)
    real, imag, top = acc_re[...], acc_im[...], acc_top[0:1, :]
    cross = [split(real + parity * next_block(real), 2), split(imag + parity * next_block(imag), 2)]
    corr = jnp.zeros_like(real)
    for a, b in ((1, 0), (0, 1), (0, 0)):
        corr = corr + (mm(inverse(a, 0), cross[0][b]) + mm(inverse(a, 1), cross[1][b]))
    corr = corr - (top + next_block(top)) * (parity * (1.0 / BLOCK))
    parts = split(jnp.concatenate([squares[0], squares[1]], axis=1), 2)
    later = mm(sums(1), parts[0]) + mm(sums(1), parts[1])
    parts = [jnp.concatenate(lanes_of(part)[::-1], axis=1) for part in parts]
    earlier = mm(sums(2), parts[0]) + mm(sums(2), parts[1])
    sums_of = lanes_of(later[0:1, :])
    whole = []
    for i in range(blocks):
        value = jnp.zeros((1, width), jnp.float32)
        for j in list(range(i + 1, blocks)) + list(range(blocks - 1 - i)):
            value = value + sums_of[j]
        whole.append(value)
    result = later + earlier + jnp.concatenate(whole, axis=1) + corr
    for i, piece in enumerate(lanes_of(result)):
        lag = i * BLOCK + lax.broadcasted_iota(jnp.int32, (BLOCK, 1), 0)
        pairs = (blocks * BLOCK - lag).astype(jnp.float32)
        out[:, i * BLOCK : (i + 1) * BLOCK] = jnp.transpose(piece / pairs)

    for c in range(3):
        sent(c, False)
        sent(c, True)


def fused(displacements):
    frames, _, atom_count = displacements.shape
    groups = lax.axis_size("frames")
    length = frames * groups
    width = atom_count // groups
    blocks = length // BLOCK
    table = tables()
    lanes = -(-3 * frames // LANES) * LANES
    f32, bf16 = jnp.float32, jnp.bfloat16
    dma = pltpu.SemaphoreType.DMA
    return pl.pallas_call(
        functools.partial(kernel, groups, atom_count * lax.axis_size("atoms")),
        out_shape=jax.ShapeDtypeStruct((width, length), f32),
        in_specs=[pl.BlockSpec(memory_space=pltpu.HBM)] * 2,
        out_specs=pl.BlockSpec(memory_space=pltpu.VMEM),
        scratch_shapes=[
            pltpu.VMEM((3, frames, atom_count), f32),
            pltpu.VMEM((3, length, width), f32),
            pltpu.VMEM((1, lanes), f32),
            pltpu.VMEM((1, lanes), f32),
            pltpu.VMEM((1, lanes), f32),
            pltpu.VMEM((groups, 1, lanes), f32),
            pltpu.VMEM(table.shape, bf16),
            pltpu.VMEM((3, length, width), f32),
            pltpu.VMEM((2, 2 * BLOCK + 16, blocks * width // 2), f32),
            pltpu.VMEM((BLOCK, blocks * width), f32),
            pltpu.VMEM((BLOCK, blocks * width), f32),
            pltpu.VMEM((8, blocks * width), f32),
            pltpu.VMEM((2, BLOCK, blocks * width // 2), f32),
            dma((3,)), dma, dma((3,)), dma((3, 2)), dma((3, 2)),
            dma, dma, dma((groups,)), dma((groups,)),
        ],
        compiler_params=pltpu.CompilerParams(
            collective_id=0, has_side_effects=True, vmem_limit_bytes=61_190_000
        ),
    )(jnp.transpose(displacements, (1, 0, 2)), jnp.asarray(table))


def fits(mesh, shape):
    groups, pairs = mesh.shape["frames"], mesh.shape["atoms"]
    length, _, atoms = shape
    if pairs != 2 or groups % 2 or atoms != pairs * groups * LANES or length != 4 * BLOCK:
        return False
    return length // groups % 8 == 0


def solution(mesh):
    def run(displacements):
        return jax.shard_map(
            fused if fits(mesh, displacements.shape) else per_device,
            mesh=mesh,
            in_specs=(P("frames", None, "atoms"),),
            out_specs=P(("atoms", "frames"), None),
            check_vma=False,
        )(displacements)

    return run
```

```python
import functools
import math

import jax
import jax.numpy as jnp
import ml_dtypes
import numpy as np
from jax import lax
from jax.experimental import pallas as pl
from jax.experimental.pallas import tpu as pltpu
from jax.sharding import PartitionSpec as P


BLOCK = 256
LANES = 128
PIECES = 4
MESH = pl.DeviceIdType.MESH


def carried_in(array, axis, combine, identity):
    count, index = (lax.axis_size(axis), lax.axis_index(axis))
    everything = lax.all_gather(array, axis)
    start = jnp.broadcast_to(jnp.asarray(identity, array.dtype), array.shape)

    def hop(k, before):
        reached = k < index
        new = combine(before, everything[k])
        return jnp.where(reached, new, before)

    return lax.fori_loop(0, count, hop, start)


def lag_table(positions):
    length = positions.shape[0]
    count = positions.shape[3]
    series = positions.reshape(length, 3 * count)
    squares = jnp.sum(positions * positions, axis=(1, 2))
    zero_row = jnp.zeros((1, count), jnp.float32)
    running = jnp.concatenate([zero_row, jnp.cumsum(squares, axis=0)], axis=0)
    head = running[length][None, :] - running[:length]
    tail = jnp.flip(running[1:], 0)
    block = min(256, length)
    frame = jnp.arange(length, dtype=jnp.int32)
    starts = jnp.arange(0, length, block, dtype=jnp.int32)

    def add_block(corr, start):
        freq = start + jnp.arange(block, dtype=jnp.int32)
        phase = frame[:, None] * freq[None, :] % (2 * length)
        angle = phase.astype(jnp.float32) * (math.pi / length)
        cosine = jnp.cos(angle)
        sine = jnp.sin(angle)
        real_part = lax.dot_general(
            series, cosine, (((0,), (0,)), ((), ())), precision=lax.Precision.HIGHEST
        )
        imag_part = lax.dot_general(
            series, sine, (((0,), (0,)), ((), ())), precision=lax.Precision.HIGHEST
        )
        power = jnp.sum(
            (real_part * real_part + imag_part * imag_part).reshape(3, count, block), axis=0
        )
        weight = jnp.where(freq == 0, 1.0, 2.0).astype(jnp.float32) / (2.0 * length)
        term = lax.dot_general(
            power * weight[None, :],
            cosine,
            (((1,), (1,)), ((), ())),
            precision=lax.Precision.HIGHEST,
        )
        return (corr + term, None)

    corr, _ = lax.scan(add_block, jnp.zeros((count, length), jnp.float32), starts)
    parity = jnp.where(frame % 2 == 0, 1.0, -1.0).astype(jnp.float32)
    highest = jnp.dot(parity, series, precision=lax.Precision.HIGHEST)
    power_top = jnp.sum((highest * highest).reshape(3, count), axis=0)
    corr = corr + power_top[:, None] * parity[None, :] / (2.0 * length)
    counts = (length - frame).astype(jnp.float32)
    return (jnp.transpose(head + tail) - 2.0 * corr) / counts[None, :]


def add_carry(earlier, later):
    return earlier + later


def per_device(displacements):
    local_frames, _, atom_count = displacements.shape
    groups = lax.axis_size("frames")
    atom_total = atom_count * lax.axis_size("atoms")
    summed = lax.psum(jnp.sum(displacements, axis=2), "atoms")
    centred = displacements - (summed / atom_total)[:, :, None]
    partial_value = jnp.cumsum(centred, axis=0)
    earlier = carried_in(partial_value[-1], "frames", add_carry, jnp.zeros_like(partial_value[-1]))
    positions = (partial_value + earlier[None]).reshape(
        local_frames, 3, groups, atom_count // groups
    )
    return lag_table(lax.all_to_all(positions, "frames", split_axis=2, concat_axis=0, tiled=True))


def tables():
    points = 2 * BLOCK
    index = np.arange(BLOCK)
    angle = 2.0 * np.pi * (np.outer(index, index) % points) / points
    forward = np.zeros((points + 16, BLOCK))
    forward[:BLOCK] = np.cos(angle)
    forward[BLOCK:points] = -np.sin(angle)
    forward[points] = 1.0 - 2.0 * (index % 2)
    weight = np.where(index == 0, 1.0, 2.0)[None, :] / points
    inverse = [-2.0 * np.cos(angle) * weight, 2.0 * np.sin(angle) * weight]
    row, col = index[:, None], index[None, :]
    sums = [col <= row, col >= row, col <= BLOCK - 1 - row]
    pieces = rounded(forward, 2)
    pieces += [part.astype(ml_dtypes.bfloat16) for part in sums]
    pieces += [part for pair in zip(*(rounded(half, 2) for half in inverse)) for part in pair]
    return np.concatenate(pieces, axis=0)


def rounded(values, terms):
    parts = []
    for _ in range(terms):
        part = values.astype(ml_dtypes.bfloat16)
        parts.append(part)
        values = values - part.astype(np.float64)
    return parts


def split(value, terms):
    parts = []
    for _ in range(terms - 1):
        part = value.astype(jnp.bfloat16)
        parts.append(part)
        value = value - part.astype(jnp.float32)
    return parts + [value.astype(jnp.bfloat16)]


def mm(a, b):
    return jnp.dot(a, b, preferred_element_type=jnp.float32)


def kernel(
    groups, atom_total, x, table, result_out,
    out, out_sem, xv, recv, mine, sibling, total, msgs, held, drift, spectrum, acc_re, acc_im, acc_top, squares,
    load_sem, const_sem, own_sem, send_sem, recv_sem, pair_send, pair_recv, msg_send, msg_recv,
):
    me, core = lax.axis_index("frames"), lax.axis_index("atoms")
    frames = x.shape[1]
    width = recv.shape[2]
    blocks = recv.shape[1] // BLOCK
    tiles = x.shape[2] // LANES

    loads = [pltpu.make_async_copy(x.at[c], xv.at[c], load_sem.at[c]) for c in range(3)]
    for load in loads:
        load.start()
    const = pltpu.make_async_copy(table, held, const_sem)
    const.start()
    tall = 2 * BLOCK + 16

    def forward(part):
        return held[part * tall : (part + 1) * tall, :]

    def sums(which):
        start = 2 * tall + which * BLOCK
        return held[start : start + BLOCK, :]

    def inverse(part, which):
        start = 2 * tall + (3 + 2 * part + which) * BLOCK
        return held[start : start + BLOCK, :]

    def peer_at(k):
        return lax.rem(me + k, groups)

    def own_copy(c):
        return pltpu.make_async_copy(
            x.at[c, :, pl.ds(pl.multiple_of(me * width, width), width)],
            recv.at[c, pl.ds(pl.multiple_of(me * frames, frames), frames), :],
            own_sem.at[c],
        )

    barrier = pltpu.get_barrier_semaphore()

    def greet(k, carry):
        pl.semaphore_signal(barrier, inc=1, device_id={"frames": peer_at(k)}, device_id_type=MESH)
        return carry

    pl.semaphore_signal(barrier, inc=1, device_id={"atoms": 1 - core}, device_id_type=MESH)
    lax.fori_loop(1, groups, greet, 0)
    pl.semaphore_wait(barrier, groups)

    half = groups // 2
    side = me // half
    spot = lax.rem(me, half)

    def send_component(c):
        def send(t, carry):
            offset = half + (1 - 2 * lax.rem(t, 2)) * ((t + 1) // 2)
            peer = peer_at(offset)
            far = lax.rem(peer // half + side, 2)
            pltpu.make_async_remote_copy(
                src_ref=x.at[c, :, pl.ds(pl.multiple_of(peer * width, width), width)],
                dst_ref=recv.at[c, pl.ds(pl.multiple_of(me * frames, frames), frames), :],
                send_sem=send_sem.at[c, far],
                recv_sem=recv_sem.at[c, far],
                device_id={"frames": peer},
                device_id_type=MESH,
            ).start()
            return carry

        lax.fori_loop(0, groups - 1, send, 0)
        own_copy(c).start()

    send_component(0)

    parts = []
    for c in range(3):
        loads[c].wait()
        part = xv[c, :, 0:LANES]
        for tile in range(1, tiles):
            part = part + xv[c, :, tile * LANES : (tile + 1) * LANES]
        parts.append(part)
    lanes = mine.shape[1]
    if lanes > 3 * frames:
        parts.append(jnp.zeros((lanes - 3 * frames, LANES), jnp.float32))
    mine[...] = jnp.sum(jnp.transpose(jnp.concatenate(parts, axis=0)), axis=0, keepdims=True)
    pair = pltpu.make_async_remote_copy(
        src_ref=mine,
        dst_ref=sibling,
        send_sem=pair_send,
        recv_sem=pair_recv,
        device_id={"atoms": 1 - core},
        device_id_type=MESH,
    )
    pair.start()
    pair.wait()
    total[...] = (mine[...] + sibling[...]) / atom_total

    def tell(k):
        return pltpu.make_async_remote_copy(
            src_ref=total,
            dst_ref=msgs.at[me],
            send_sem=msg_send.at[k],
            recv_sem=msg_recv.at[k],
            device_id={"frames": peer_at(k)},
            device_id_type=MESH,
        )

    def tell_start(k, carry):
        tell(k).start()
        return carry

    lax.fori_loop(1, groups, tell_start, 0)
    send_component(1)
    send_component(2)
    msgs[pl.ds(me, 1)] = total[...][None]

    acc_re[...] = jnp.zeros_like(acc_re)
    acc_im[...] = jnp.zeros_like(acc_im)
    acc_top[...] = jnp.zeros_like(acc_top)
    squares[...] = jnp.zeros_like(squares)
    const.wait()

    def heard(k, carry):
        source = lax.rem(me + groups - k, groups)
        pltpu.make_async_remote_copy(
            src_ref=total,
            dst_ref=msgs.at[source],
            send_sem=msg_send.at[k],
            recv_sem=msg_recv.at[k],
            device_id={"frames": source},
            device_id_type=MESH,
        ).wait()
        return carry

    lax.fori_loop(1, groups, heard, 0)

    def spread(b, carry):
        column = jnp.transpose(jnp.broadcast_to(msgs[pl.ds(b, 1)][0], (LANES, lanes)))
        for c in range(3):
            drift[c, pl.ds(pl.multiple_of(b * frames, frames), frames), :] = column[
                c * frames : (c + 1) * frames
            ]
        return carry

    lax.fori_loop(0, groups, spread, 0)

    def several(c, far):
        return recv.at[c, pl.ds(0, (half if far else half - 1) * frames), :]

    def sent(c, far):
        gone = several(c, far)
        pltpu.make_async_copy(gone, gone, send_sem.at[c, int(far)]).wait()

    def arrived(c, far):
        came = several(c, far)
        pltpu.make_async_copy(came, came, recv_sem.at[c, int(far)]).wait()

    def lanes_of(value):
        return [value[:, i : i + width] for i in range(0, value.shape[1], width)]

    def transform(c, which):
        pieces = []
        for i in range(blocks // 2):
            at = pl.ds(pl.multiple_of((which * (blocks // 2) + i) * BLOCK, BLOCK), BLOCK)
            pieces.append(recv[c, at, :] - drift[c, at, :])
        high, low = split(jnp.concatenate(pieces, axis=1), 2)
        running = mm(sums(0), high) + mm(sums(0), low)
        first, second = lanes_of(running[BLOCK - 1 : BLOCK, :])
        later = jnp.full((1, 1), which, jnp.int32).astype(jnp.float32)
        sooner = 1.0 - later
        shift = jnp.concatenate([-sooner * (first + second), later * first - sooner * second], axis=1)
        positions = running + shift
        squares[which] += positions * positions
        high, low = split(positions, 2)
        spectrum[which] = mm(forward(0), high) + (mm(forward(0), low) + mm(forward(1), high))

    def spectra(at):
        return lanes_of(spectrum[0, at, :]) + lanes_of(spectrum[1, at, :])

    def component(c, carry):
        own_copy(c).wait()
        arrived(c, False)
        transform(c, side)
        arrived(c, True)
        transform(c, 1 - side)

        def rows(r, inner):
            at = pl.ds(pl.multiple_of(r * 8, 8), 8)
            re = spectra(at)
            im = spectra(pl.ds(pl.multiple_of(BLOCK + r * 8, 8), 8))
            for d in range(blocks):
                here = slice(d * width, (d + 1) * width)
                real = acc_re[at, here]
                imag = acc_im[at, here]
                for i in range(blocks - d):
                    j = i + d
                    real = real + (re[i] * re[j] + im[i] * im[j])
                    if d:
                        imag = imag + (re[i] * im[j] - im[i] * re[j])
                acc_re[at, here] = real
                if d:
                    acc_im[at, here] = imag
            return inner

        lax.fori_loop(0, BLOCK // 8, rows, 0, unroll=4)
        top = spectra(pl.ds(2 * BLOCK, 8))
        for d in range(blocks):
            here = slice(d * width, (d + 1) * width)
            value = acc_top[:, here]
            for i in range(blocks - d):
                value = value + top[i] * top[i + d]
            acc_top[:, here] = value
        return carry

    lax.fori_loop(0, 3, component, 0)

    def next_block(value):
        return jnp.concatenate([value[:, width:], jnp.zeros_like(value[:, :width])], axis=1)

    parity = (1 - 2 * (lax.broadcasted_iota(jnp.int32, (BLOCK, 1), 0) % 2)).astype(jnp.float32)
    real, imag, top = acc_re[...], acc_im[...], acc_top[0:1, :]
    cross = [split(real + parity * next_block(real), 2), split(imag + parity * next_block(imag), 2)]
    corr = jnp.zeros_like(real)
    for a, b in ((1, 0), (0, 1), (0, 0)):
        corr = corr + (mm(inverse(a, 0), cross[0][b]) + mm(inverse(a, 1), cross[1][b]))
    corr = corr - (top + next_block(top)) * (parity * (1.0 / BLOCK))
    parts = split(jnp.concatenate([squares[0], squares[1]], axis=1), 2)
    later = mm(sums(1), parts[0]) + mm(sums(1), parts[1])
    parts = [jnp.concatenate(lanes_of(part)[::-1], axis=1) for part in parts]
    earlier = mm(sums(2), parts[0]) + mm(sums(2), parts[1])
    sums_of = lanes_of(later[0:1, :])
    whole = []
    for i in range(blocks):
        value = jnp.zeros((1, width), jnp.float32)
        for j in list(range(i + 1, blocks)) + list(range(blocks - 1 - i)):
            value = value + sums_of[j]
        whole.append(value)
    result = later + earlier + jnp.concatenate(whole, axis=1) + corr
    leaving = []
    for i, piece in enumerate(lanes_of(result)):
        lag = i * BLOCK + lax.broadcasted_iota(jnp.int32, (BLOCK, 1), 0)
        pairs = (blocks * BLOCK - lag).astype(jnp.float32)
        out[:, i * BLOCK : (i + 1) * BLOCK] = jnp.transpose(piece / pairs)
        leave = pltpu.make_async_copy(
            out.at[:, pl.ds(i * BLOCK, BLOCK)], result_out.at[:, pl.ds(i * BLOCK, BLOCK)], out_sem.at[i]
        )
        leave.start()
        leaving.append(leave)

    for c in range(3):
        sent(c, False)
        sent(c, True)
    for leave in leaving:
        leave.wait()


def fused(displacements):
    frames, _, atom_count = displacements.shape
    groups = lax.axis_size("frames")
    length = frames * groups
    width = atom_count // groups
    blocks = length // BLOCK
    table = tables()
    lanes = -(-3 * frames // LANES) * LANES
    f32, bf16 = jnp.float32, jnp.bfloat16
    dma = pltpu.SemaphoreType.DMA
    result = pl.pallas_call(
        functools.partial(kernel, groups, atom_count * lax.axis_size("atoms")),
        out_shape=jax.ShapeDtypeStruct((width, length), f32),
        in_specs=[pl.BlockSpec(memory_space=pltpu.HBM)] * 2,
        out_specs=pl.BlockSpec(memory_space=pltpu.HBM),
        scratch_shapes=[
            pltpu.VMEM((width, length), f32),
            dma((blocks,)),
            pltpu.VMEM((3, frames, atom_count), f32),
            pltpu.VMEM((3, length, width), f32),
            pltpu.VMEM((1, lanes), f32),
            pltpu.VMEM((1, lanes), f32),
            pltpu.VMEM((1, lanes), f32),
            pltpu.VMEM((groups, 1, lanes), f32),
            pltpu.VMEM(table.shape, bf16),
            pltpu.VMEM((3, length, width), f32),
            pltpu.VMEM((2, 2 * BLOCK + 16, blocks * width // 2), f32),
            pltpu.VMEM((BLOCK, blocks * width), f32),
            pltpu.VMEM((BLOCK, blocks * width), f32),
            pltpu.VMEM((8, blocks * width), f32),
            pltpu.VMEM((2, BLOCK, blocks * width // 2), f32),
            dma((3,)), dma, dma((3,)), dma((3, 2)), dma((3, 2)),
            dma, dma, dma((groups,)), dma((groups,)),
        ],
        compiler_params=pltpu.CompilerParams(
            collective_id=0, has_side_effects=True, vmem_limit_bytes=60 * 1024 * 1024
        ),
    )(jnp.transpose(displacements, (1, 0, 2)), jnp.asarray(table))
    return pl.pallas_call(
        deliver,
        out_shape=jax.ShapeDtypeStruct((width, length), f32),
        in_specs=[pl.BlockSpec(memory_space=pltpu.HBM)],
        out_specs=pl.BlockSpec(memory_space=pltpu.HBM),
        scratch_shapes=[pltpu.VMEM((width, length), f32), dma((PIECES,)), dma((PIECES,))],
    )(result)


def deliver(source, target, held, come, go):
    rows = source.shape[0] // PIECES
    here = [pl.ds(i * rows, rows) for i in range(PIECES)]
    inward = [
        pltpu.make_async_copy(source.at[at, :], held.at[at, :], come.at[i]) for i, at in enumerate(here)
    ]
    outward = [
        pltpu.make_async_copy(held.at[at, :], target.at[at, :], go.at[i]) for i, at in enumerate(here)
    ]
    for copy in inward:
        copy.start()
    for before, after in zip(inward, outward):
        before.wait()
        after.start()
    for copy in outward:
        copy.wait()


def fits(mesh, shape):
    groups, pairs = mesh.shape["frames"], mesh.shape["atoms"]
    length, _, atoms = shape
    if pairs != 2 or groups % 2 or atoms != pairs * groups * LANES or length != 4 * BLOCK:
        return False
    return length // groups % 8 == 0


def solution(mesh):
    def run(displacements):
        return jax.shard_map(
            fused if fits(mesh, displacements.shape) else per_device,
            mesh=mesh,
            in_specs=(P("frames", None, "atoms"),),
            out_specs=P(("atoms", "frames"), None),
            check_vma=False,
        )(displacements)

    return run
```
